512 devices in a mesh: blk: 16 (over x, y_lo, core), lane: 32 (over z, y_hi).
Axes of the slice: x: 4, y: 4 (y_hi: 2, y_lo: 2; y = y_hi * 2 + y_lo), z: 16, core: 2. Of those that a mesh axis runs over, the one named last changes fastest.
Arguments:
- positions: float32 [3, 12288], P(None, ('blk', 'lane')), may hold values from -4 to 4
- velocities: float32 [3, 12288], P(None, ('blk', 'lane')), may hold values from -3 to 3
- masses: float32 [12288], P(('blk', 'lane')), may hold values from 0.2 to 5
- tangents: float32 [6, 12288, 128], P(None, ('blk', 'lane')), may hold values from -14 to 14
Outputs:
- new_positions: float32 [3, 12288], P(None, ('blk', 'lane'))
- new_velocities: float32 [3, 12288], P(None, ('blk', 'lane'))
- basis: float32 [6, 12288, 128], P(None, ('blk', 'lane'))
- growth: float32 [128, 128], replicated
The draws below stay inside these ranges and needn't reach their ends.
All inputs are finite; a program needn't handle non-finite values.
Results may differ from the reference program's by a relative error of at most 0.0003.
Values sent between devices are 32-bit elements; how exact they have to be, the bound alone decides.
A program may use at most 64 MiB of HBM per device.

```python
import math
import jax
import jax.numpy as jnp
from jax import lax

K = 128
STARS = 12288


def star_positions(key):
    return jnp.clip(jax.random.normal(jax.random.fold_in(key, 11), (3, STARS), jnp.float32), -4.0, 4.0)


def draw_positions(key, part):
    return star_positions(key)


def draw_tangents(key, part):
    places = star_positions(key)
    noise = jnp.clip(jax.random.normal(key, (6, STARS, K + 1), jnp.float32), -5.0, 5.0)
    rough = noise[:, :, 1:] + 0.6 * noise[:, :, :-1]
    waves = 0.8 * jax.random.normal(jax.random.fold_in(key, 21), (6, 3, K), jnp.float32)
    phases = jax.random.uniform(jax.random.fold_in(key, 22), (6, K), jnp.float32, -math.pi, math.pi)
    argument = places[0][None, :, None] * waves[:, 0][:, None, :]
    argument = argument + places[1][None, :, None] * waves[:, 1][:, None, :]
    argument = argument + places[2][None, :, None] * waves[:, 2][:, None, :]
    smooth = 1.5 * jnp.sin(argument + phases[:, None, :])
    return rough + smooth


def level_of(rng, extent, split, least, high):
    def one(position, parts):
        draws = jax.random.uniform(jax.random.fold_in(jax.random.fold_in(rng, 6), position), (parts,), jnp.float32, least / len(split), high / len(split))
        return jnp.repeat(jnp.exp(draws), extent[position] // parts).reshape((-1,) + (1,) * (len(extent) - position - 1))

    level = one(*split[0])
    for cut in split[1:]:
        level = level * one(*cut)
    return level


def bell_draw(key, extent, scale, most, split=(), kind=jnp.bfloat16):
    array = jax.random.normal(key, extent, jnp.float32) * scale
    if len(split) > 0:
        array = level_of(key, extent, split, -0.22, 0.18) * array
    return jnp.clip(array, min=-most, max=most).astype(kind)


def setup_inputs(seed: int = 0) -> dict:
    keys = jax.random.split(jax.random.key(seed), 5)
    positions = draw_positions(jax.random.fold_in(keys[4], 71), 0)
    velocities = bell_draw(keys[1], (3, STARS), 0.5, 3.0, ((1, 512),), jnp.float32)
    masses = jnp.clip(jnp.exp(math.log(5.0) - 3.218876 * jax.random.uniform(keys[2], (STARS,), jnp.float32) ** level_of(keys[2], (STARS,), ((0, 512),), -0.2, 0.2)), 0.2, 5.0)
    tangents = draw_tangents(jax.random.fold_in(keys[4], 71), 0)
    return {"positions": positions, "velocities": velocities, "masses": masses, "tangents": tangents}


STEP = 0.0625
SOFT = 0.0025

def pull_block(targets, pos_half, mass, dx_half):
    offsets = pos_half[:, None, :] - targets[:, :, None]
    squared = lax.optimization_barrier(jnp.sum(offsets * offsets, axis=0)) + SOFT
    inverse = lax.rsqrt(squared)
    near_weight = mass[None, :] * inverse * inverse * inverse
    tide_weight = near_weight / squared
    acceleration = lax.optimization_barrier(jnp.sum(near_weight[None] * offsets, axis=2))
    identity = jnp.eye(3, dtype=jnp.float32)
    kernel = identity[:, None, :, None] * near_weight[None, :, None, :] - 3.0 * tide_weight[None, :, None, :] * offsets[:, :, None, :] * jnp.transpose(offsets, (1, 0, 2))[None]
    row_sums = lax.optimization_barrier(jnp.sum(kernel, axis=3))
    count = targets.shape[1]
    stacked = dx_half.reshape(-1, dx_half.shape[2])
    product = jnp.einsum('aij,jk->aik', kernel.reshape(3, count, -1).astype(jnp.float32), stacked.astype(jnp.float32), precision=lax.Precision.HIGHEST, preferred_element_type=jnp.float32)
    return (acceleration, row_sums, product)

def reference(positions, velocities, masses, tangents):
    half_step = 0.5 * STEP
    mass = masses / STARS
    pos_half = positions + half_step * velocities
    dx_half = tangents[:3] + half_step * tangents[3:]
    block_size = math.gcd(STARS, 128)
    blocks = STARS // block_size
    target_blocks = jnp.transpose(pos_half.reshape(3, blocks, block_size), (1, 0, 2))

    def one_block(targets):
        return pull_block(targets, pos_half, mass, dx_half)
    accel_blocks, row_blocks, pull_blocks = lax.map(one_block, target_blocks)
    acceleration = jnp.transpose(accel_blocks, (1, 0, 2)).reshape(3, STARS)
    row_sums = jnp.transpose(row_blocks, (1, 3, 0, 2)).reshape(3, 3, STARS)
    tangent_pull = jnp.transpose(pull_blocks, (1, 0, 2, 3)).reshape(3, STARS, K)
    tangent_pull = tangent_pull - lax.optimization_barrier(jnp.sum(row_sums[:, :, :, None] * dx_half[None], axis=1))
    new_velocities = velocities + STEP * acceleration
    dv_new = tangents[3:] + STEP * tangent_pull
    new_positions = pos_half + half_step * new_velocities
    dx_new = dx_half + half_step * dv_new
    matrix = jnp.concatenate([dx_new, dv_new], axis=0).reshape(-1, K)
    factor_q, factor_r = jnp.linalg.qr(matrix)
    signs = jnp.sign(jnp.diagonal(factor_r))
    factor_r = factor_r * signs[:, None]
    factor_q = factor_q * signs[None, :]
    total = jnp.float32(6 * STARS)
    growth = factor_r / jnp.sqrt(total)
    basis = (factor_q * jnp.sqrt(total)).reshape(6, STARS, K)
    return (new_positions, new_velocities, basis, growth)
```

```python
import functools

import jax
import jax.numpy as jnp
from jax import lax
from jax.experimental import pallas as pl
from jax.experimental.pallas import tpu as pltpu
from jax.sharding import PartitionSpec as P

STEP = 0.0625
SOFT = 0.0025
HALF = 0.5 * STEP
MESH = pl.DeviceIdType.MESH
HIGHEST = lax.Precision.HIGHEST
Y = 4


def lane_iota(shape):
    return lax.broadcasted_iota(jnp.int32, shape, 1)


def pack_lanes(tiles, width):
    pieces = [None] * ((len(tiles) * width + 127) // 128)
    lanes = lane_iota((8, 128))

    def put(index, value):
        pieces[index] = value if pieces[index] is None else pieces[index] + value

    for index, tile in enumerate(tiles):
        chunk, offset = divmod(index * width, 128)
        turned = pltpu.roll(tile, offset, 1) if offset else tile
        if offset + width > 128:
            put(chunk, jnp.where(lanes >= offset, turned, 0.0))
            put(chunk + 1, jnp.where(lanes < offset, turned, 0.0))
        else:
            put(chunk, turned)
    return pieces


def step_kernel(
    xs, zs, n, total,
    pos_ref, vel_ref, mass_ref, tan_ref,
    gram_ref, mat_ref, npos_ref, nvel_ref,
    row_z, row_p, dx_buf, src, tgt, k_hi, k_lo, dx_b,
    ext_send, ext_recv, out_send, out_recv,
    g_own, g_sib, g_half, g_plane, g_mine, g_line, g_all,
    pz_send, pz_recv, pp_send, pp_recv, ps_send, ps_recv,
    up_send, up_recv, dn_send, dn_recv, sh_send, sh_recv,
    ex_send, ex_recv, rs_send, rs_recv, gs_send, gs_recv,
):
    blk, lane = lax.axis_index("blk"), lax.axis_index("lane")
    core = lax.rem(blk, 2)
    px = blk // 4
    py = lax.rem(lane, 2) * 2 + lax.rem(blk // 2, 2)
    z = lane // 2
    planes = xs * Y
    targets = planes * n
    sources = 2 * zs * n
    up_steps, dn_steps = zs // 2, (zs - 1) // 2

    def plane_peer(i, j):
        ox, oy = lax.rem(px + i, xs), lax.rem(py + j, Y)
        return (ox * 4 + lax.rem(oy, 2) * 2 + core, z * 2 + oy // 2), ox * Y + oy

    def plane_back(i, j):
        return lax.rem(xs - i, xs) * Y + lax.rem(Y - j, Y)

    def line_peer(r):
        return (blk, lax.rem(z + r, zs) * 2 + lax.rem(lane, 2))

    sibling = (blk + 1 - 2 * core, lane)
    here = px * Y + py

    def remote(source, target, send_sem, recv_sem, device):
        return pltpu.make_async_remote_copy(
            src_ref=source, dst_ref=target, send_sem=send_sem, recv_sem=recv_sem,
            device_id=device, device_id_type=MESH,
        )

    barrier = pltpu.get_barrier_semaphore()
    for r in range(1, zs):
        pl.semaphore_signal(barrier, inc=1, device_id=line_peer(r), device_id_type=MESH)
    for t in range(1, planes):
        pl.semaphore_signal(barrier, inc=1, device_id=plane_peer(t // Y, t % Y)[0], device_id_type=MESH)
    pl.semaphore_signal(barrier, inc=1, device_id=sibling, device_id_type=MESH)

    pos_half = pos_ref[...] + HALF * vel_ref[...]
    row_z[0, 0] = jnp.zeros((8, 128), jnp.float32)
    row_z[0, 0, 0:3, 0:n] = pos_half
    row_z[0, 0, 3:4, 0:n] = mass_ref[...] / total
    row_p[0] = row_z[0, 0]
    dx_half = tan_ref[0:3] + HALF * tan_ref[3:6]
    dx_buf[:, 0, 0] = dx_half
    pl.semaphore_wait(barrier, zs - 1 + planes - 1 + 1)

    for r in range(1, zs):
        remote(row_z.at[0, 0], row_z.at[0, zs - r], pz_send, pz_recv, line_peer(r)).start()
    for t in range(1, planes):
        remote(row_z.at[0, 0], row_p.at[plane_back(t // Y, t % Y)], pp_send, pp_recv, plane_peer(t // Y, t % Y)[0]).start()

    def up_copy(s):
        return remote(
            dx_buf.at[:, 0, (zs - s + 1) % zs], dx_buf.at[:, 0, zs - s],
            up_send.at[s - 1], up_recv.at[s - 1], line_peer(1),
        )

    def dn_copy(s):
        return remote(
            dx_buf.at[:, 0, s - 1], dx_buf.at[:, 0, s],
            dn_send.at[s - 1], dn_recv.at[s - 1], line_peer(zs - 1),
        )

    def share(r):
        return remote(dx_buf.at[:, 0, r], dx_buf.at[:, 1, r], sh_send.at[r], sh_recv.at[r], sibling)

    def advance(s):
        up_copy(s).wait_recv()
        if s + 1 <= up_steps:
            up_copy(s + 1).start()
        if s <= dn_steps:
            dn_copy(s).wait_recv()
            if s + 1 <= dn_steps:
                dn_copy(s + 1).start()
        share(zs - s).start()
        if s <= dn_steps:
            share(s).start()

    up_copy(1).start()
    if dn_steps:
        dn_copy(1).start()
    share(0).start()

    remote(row_z.at[0, pl.ds(1, zs - 1)], row_z.at[0, pl.ds(1, zs - 1)], pz_send, pz_recv, sibling).wait_recv()
    line_share = remote(row_z.at[0], row_z.at[1], ps_send, ps_recv, sibling)
    line_share.start()
    remote(row_p.at[pl.ds(1, planes - 1)], row_p.at[pl.ds(1, planes - 1)], pp_send, pp_recv, sibling).wait_recv()
    for c, piece in enumerate(pack_lanes([row_p[t] for t in range(planes)], n)):
        tgt[c * 128:(c + 1) * 128, 0:8] = piece.T
    advance(1)
    line_share.wait_recv()
    tiles = [row_z[h, r] for h in range(2) for r in range(zs)]
    for c, piece in enumerate(pack_lanes(tiles, n)):
        src[:, c * 128:(c + 1) * 128] = piece

    subs = 2 * n // 16
    lanes16 = lane_iota((16, 128))

    def pair_block(b, _):
        pair, sub = b // subs, lax.rem(b, subs)
        base = pair * (6 * n) + sub * 16
        place = tgt[pl.ds(pl.multiple_of(b * 16, 16), 16), 0:8]
        own = [jnp.broadcast_to(place[:, a:a + 1], (16, 128)) for a in range(3)]
        sums = [None] * 9
        for c in range(sources // 128):
            columns = pl.ds(c * 128, 128)
            d = [src[a:a + 1, columns] - own[a] for a in range(3)]
            squared = d[0] * d[0] + d[1] * d[1] + d[2] * d[2] + SOFT
            inverse = lax.rsqrt(squared)
            inverse2 = inverse * inverse
            near = src[3:4, columns] * inverse * inverse2
            tide = 3.0 * near * inverse2
            td = [tide * d[a] for a in range(3)]
            part = {}
            for a in range(3):
                for e in range(a, 3):
                    product = td[a] * d[e]
                    part[a, e] = near - product if a == e else -product
            terms = [near * d[a] for a in range(3)] + [part[a, e] for a in range(3) for e in range(a, 3)]
            sums = [t if s is None else s + t for s, t in zip(sums, terms)]
            for a in range(3):
                for e in range(a, 3):
                    high = part[a, e].astype(jnp.bfloat16)
                    low = (part[a, e] - high.astype(jnp.float32)).astype(jnp.bfloat16)
                    for f, g in {(a, e), (e, a)}:
                        where = (pl.ds(pl.multiple_of(base + f * 2 * n, 16), 16), pl.ds(g * sources + c * 128, 128))
                        k_hi[where] = high
                        k_lo[where] = low
        tile = jnp.zeros((16, 128), jnp.float32)
        for k, s in enumerate(sums):
            tile = jnp.where(lanes16 == k, jnp.sum(s, axis=1, keepdims=True), tile)
        ext_send[pl.ds(pl.multiple_of(b * 16, 16), 16), :] = tile
        return 0

    blocks = targets // 16
    slots = max(up_steps - 1, 1)
    done = 0
    for s in range(2, up_steps + 1):
        upto = blocks * (s - 1) // slots
        lax.fori_loop(done, upto, pair_block, 0)
        done = upto
        advance(s)

    for t in range(1, planes):
        back = plane_back(t // Y, t % Y)
        remote(
            ext_send.at[pl.ds(t * n, n)], ext_recv.at[back - 1], ex_send, ex_recv, plane_peer(t // Y, t % Y)[0]
        ).start()

    for r in range(zs):
        share(r).wait_recv()
    for b in range(3):
        for h in range(2):
            block = dx_buf[b, h].reshape(zs * n, 128)
            high = block.astype(jnp.bfloat16)
            low = (block - high.astype(jnp.float32)).astype(jnp.bfloat16)
            start = b * sources + h * zs * n
            dx_b[start:start + zs * n, 0:128] = high
            dx_b[start:start + zs * n, 128:256] = low

    group = 4
    rows = group * 3 * n

    def pull_group(g, _):
        where = pl.ds(pl.multiple_of(g * rows, 16), rows)
        first = jnp.dot(k_hi[where, :], dx_b[...], preferred_element_type=jnp.float32)
        second = jnp.dot(k_lo[where, :], dx_b[:, 0:128], preferred_element_type=jnp.float32)
        pulled = first[:, 0:128] + (first[:, 128:256] + second)
        out_send[pl.ds(g * (group // 2), group // 2)] = pulled.reshape(group // 2, 3, 2, n, 128)
        for u in range(group):
            t = g * group + u
            i, j = t // Y, lax.rem(t, Y)

            @pl.when(t != 0)
            def _():
                remote(
                    out_send.at[t // 2, :, lax.rem(t, 2)], out_recv.at[plane_back(i, j) - 1],
                    rs_send, rs_recv, plane_peer(i, j)[0],
                ).start()

        return 0

    lax.fori_loop(0, planes // group, pull_group, 0)

    remote(ext_recv, ext_recv, ex_send, ex_recv, sibling).wait_recv()
    extra = ext_send[0:n, :]
    for t in range(planes - 1):
        extra = extra + ext_recv[t]
    acceleration = extra.T[0:3, :]
    new_velocities = vel_ref[...] + STEP * acceleration
    nvel_ref[...] = new_velocities
    npos_ref[...] = pos_half + HALF * new_velocities
    index = {}
    for a in range(3):
        for e in range(a, 3):
            index[a, e] = index[e, a] = 3 + len(set(index.values()))
    offset = []
    for a in range(3):
        taken = 0.0
        for e in range(3):
            taken = taken + extra[:, index[a, e]:index[a, e] + 1] * dx_buf[e, 0, 0]
        offset.append(taken)

    remote(out_recv, out_recv, rs_send, rs_recv, sibling).wait_recv()
    for a in range(3):
        pulled = out_send[0, a, 0]
        for t in range(planes - 1):
            pulled = pulled + out_recv[t, a]
        dv_new = tan_ref[3 + a] + STEP * (pulled - offset[a])
        mat_ref[3 + a] = dv_new
        mat_ref[a] = dx_buf[a, 0, 0] + HALF * dv_new
    matrix = mat_ref[...].reshape(6 * n, 128)
    gram = lax.dot_general(
        matrix, matrix, (((0,), (0,)), ((), ())), precision=HIGHEST, preferred_element_type=jnp.float32
    )

    part_rows = 64 // planes
    g_own[...] = gram.reshape(2, planes, part_rows, 128)
    first = remote(g_own.at[1 - core], g_sib, gs_send.at[0], gs_recv.at[0], sibling)
    first.start()
    first.wait_recv()
    g_half[...] = g_own[core] + g_sib[...]
    for t in range(1, planes):
        device, place = plane_peer(t // Y, t % Y)
        remote(
            g_half.at[place], g_plane.at[plane_back(t // Y, t % Y) - 1], gs_send.at[1], gs_recv.at[1], device
        ).start()
    remote(g_plane, g_plane, gs_send.at[1], gs_recv.at[1], sibling).wait_recv()
    mine = g_half[here]
    for t in range(planes - 1):
        mine = mine + g_plane[t]
    g_mine[...] = mine
    for r in range(1, zs):
        remote(g_mine, g_line.at[zs - r - 1], gs_send.at[2], gs_recv.at[2], line_peer(r)).start()
    remote(g_line, g_line, gs_send.at[2], gs_recv.at[2], sibling).wait_recv()
    for r in range(zs - 1):
        mine = mine + g_line[r]
    g_all[core, here] = mine / (6.0 * total)
    for t in range(1, planes):
        remote(
            g_all.at[core, here], g_all.at[core, here], gs_send.at[3], gs_recv.at[3], plane_peer(t // Y, t % Y)[0]
        ).start()
    some = g_all.at[core, pl.ds(0, planes - 1)]
    remote(some, some, gs_send.at[3], gs_recv.at[3], sibling).wait_recv()
    last = remote(g_all.at[core], g_all.at[core], gs_send.at[4], gs_recv.at[4], sibling)
    last.start()
    last.wait_recv()
    gram_ref[...] = g_all[...].reshape(128, 128)

    remote(row_z.at[0, pl.ds(1, zs - 1)], row_z.at[0, pl.ds(1, zs - 1)], pz_send, pz_recv, sibling).wait_send()
    remote(row_p.at[pl.ds(1, planes - 1)], row_p.at[pl.ds(1, planes - 1)], pp_send, pp_recv, sibling).wait_send()
    line_share.wait_send()
    for s in range(1, up_steps + 1):
        up_copy(s).wait_send()
        if s <= dn_steps:
            dn_copy(s).wait_send()
    for r in range(zs):
        share(r).wait_send()
    remote(ext_recv, ext_recv, ex_send, ex_recv, sibling).wait_send()
    remote(out_recv, out_recv, rs_send, rs_recv, sibling).wait_send()
    first.wait_send()
    remote(g_plane, g_plane, gs_send.at[1], gs_recv.at[1], sibling).wait_send()
    remote(g_line, g_line, gs_send.at[2], gs_recv.at[2], sibling).wait_send()
    remote(some, some, gs_send.at[3], gs_recv.at[3], sibling).wait_send()
    last.wait_send()


def factor_kernel(gram_ref, mat_ref, npos_ref, nvel_ref, pos_out, vel_out, basis_out, growth_out):
    k = gram_ref.shape[0]
    count = k // 8
    pos_out[...] = npos_ref[...]
    vel_out[...] = nvel_ref[...]
    lanes = lane_iota((8, k))
    rows = lax.broadcasted_iota(jnp.int32, (8, k), 0)
    a = [gram_ref[8 * i:8 * i + 8, :] for i in range(count)]
    q = [jnp.where(lanes == rows + 8 * i, 1.0, 0.0) for i in range(count)]
    full = lambda row: jnp.broadcast_to(row, (8, k))
    inverse_rows = []
    for b in range(count):
        c = {
            i: [jnp.broadcast_to(a[i][:, 8 * b + e:8 * b + e + 1], (8, k)) for e in range(8)]
            for i in range(b, count)
        }
        scale = jnp.ones((8, k), jnp.float32)
        for r in range(8):
            arow, qrow = full(a[b][r:r + 1, :]), full(q[b][r:r + 1, :])
            crow = {e: full(c[b][e][r:r + 1, :]) for e in range(r, 8)}
            scale = jnp.where(rows == r, lax.rsqrt(crow[r]), scale)
            inverse = 1.0 / crow[r]
            for i in range(b, count):
                m = c[i][r] * inverse
                if i == b:
                    m = jnp.where(rows > r, m, 0.0)
                a[i] = a[i] - m * arow
                q[i] = q[i] - m * qrow
                for e in range(r + 1, 8):
                    c[i][e] = c[i][e] - m * crow[e]
        growth_out[8 * b:8 * b + 8, :] = jnp.where(lanes >= rows + 8 * b, a[b] * scale, 0.0)
        inverse_rows.append(q[b] * scale)
    inverse = jnp.concatenate(inverse_rows, axis=0)
    matrix = mat_ref[...].reshape(-1, k)
    basis = lax.dot_general(
        matrix, inverse, (((1,), (1,)), ((), ())), precision=HIGHEST, preferred_element_type=jnp.float32
    )
    basis_out[...] = basis.reshape(basis_out.shape)


def body(positions, velocities, masses, tangents):
    n, k = positions.shape[1], tangents.shape[2]
    xs, zs = lax.axis_size("blk") // 4, lax.axis_size("lane") // 2
    planes = xs * Y
    total = float(n * planes * zs * 2)
    targets, sources = planes * n, 2 * zs * n
    f32, bf16 = jnp.float32, jnp.bfloat16
    vmem = pl.BlockSpec(memory_space=pltpu.VMEM)
    dma = pltpu.SemaphoreType.DMA
    part_rows = 64 // planes
    scratch = [
        pltpu.VMEM((2, zs, 8, 128), f32),
        pltpu.VMEM((planes, 8, 128), f32),
        pltpu.VMEM((3, 2, zs, n, k), f32),
        pltpu.VMEM((8, sources), f32),
        pltpu.VMEM(((targets + 127) // 128 * 128, 128), f32),
        pltpu.VMEM((3 * targets, 3 * sources), bf16),
        pltpu.VMEM((3 * targets, 3 * sources), bf16),
        pltpu.VMEM((3 * sources, 2 * k), bf16),
        pltpu.VMEM((targets, 128), f32),
        pltpu.VMEM((planes - 1, n, 128), f32),
        pltpu.VMEM((planes // 2, 3, 2, n, k), f32),
        pltpu.VMEM((planes - 1, 3, n, k), f32),
        pltpu.VMEM((2, planes, part_rows, k), f32),
        pltpu.VMEM((planes, part_rows, k), f32),
        pltpu.VMEM((planes, part_rows, k), f32),
        pltpu.VMEM((planes - 1, part_rows, k), f32),
        pltpu.VMEM((part_rows, k), f32),
        pltpu.VMEM((zs - 1, part_rows, k), f32),
        pltpu.VMEM((2, planes, part_rows, k), f32),
        dma, dma, dma, dma, dma, dma,
        dma((zs // 2,)), dma((zs // 2,)), dma((zs // 2,)), dma((zs // 2,)),
        dma((zs,)), dma((zs,)),
        dma, dma, dma, dma, dma((5,)), dma((5,)),
    ]
    gram, matrix, npos, nvel = pl.pallas_call(
        functools.partial(step_kernel, xs, zs, n, total),
        out_shape=[
            jax.ShapeDtypeStruct((k, k), f32),
            jax.ShapeDtypeStruct((6, n, k), f32),
            jax.ShapeDtypeStruct((3, n), f32),
            jax.ShapeDtypeStruct((3, n), f32),
        ],
        in_specs=[vmem] * 4,
        out_specs=[vmem] * 4,
        scratch_shapes=scratch,
        compiler_params=pltpu.CompilerParams(
            collective_id=0, has_side_effects=True, vmem_limit_bytes=40 * 1024 * 1024
        ),
    )(positions, velocities, masses.reshape(1, n), tangents)
    npos, nvel, basis, growth = pl.pallas_call(
        factor_kernel,
        out_shape=[
            jax.ShapeDtypeStruct((3, n), f32),
            jax.ShapeDtypeStruct((3, n), f32),
            jax.ShapeDtypeStruct((6, n, k), f32),
            jax.ShapeDtypeStruct((k, k), f32),
        ],
        in_specs=[vmem] * 4,
        out_specs=[vmem] * 4,
        compiler_params=pltpu.CompilerParams(vmem_limit_bytes=40 * 1024 * 1024),
    )(gram, matrix, npos, nvel)
    return (npos, nvel, basis, growth)


def solution(mesh):
    return jax.shard_map(
        body,
        mesh=mesh,
        in_specs=(
            P(None, ("blk", "lane")),
            P(None, ("blk", "lane")),
            P(("blk", "lane")),
            P(None, ("blk", "lane"), None),
        ),
        out_specs=(
            P(None, ("blk", "lane")),
            P(None, ("blk", "lane")),
            P(None, ("blk", "lane"), None),
            P(),
        ),
        check_vma=False,
    )
```

```python
import functools

import jax
import jax.numpy as jnp
from jax import lax
from jax.experimental import pallas as pl
from jax.experimental.pallas import tpu as pltpu
from jax.sharding import PartitionSpec as P

STEP = 0.0625
SOFT = 0.0025
HALF = 0.5 * STEP
MESH = pl.DeviceIdType.MESH
HIGHEST = lax.Precision.HIGHEST
Y = 4


RING = {
    16: (
        {0: (3, -3, 1, -1), 3: (6, 2, 4), -3: (-6, -2, -4), 6: (8, 5, 7), -6: (-5, -7)},
        ((3, -3, 1, -1), (6, -6, 2, -2, 4, -4), (5, -5, 7, -7, 8)),
    ),
    4: ({0: (1, -1), 1: (2,)}, ((1,), (-1,), (2,))),
}


def lane_iota(shape):
    return lax.broadcasted_iota(jnp.int32, shape, 1)


def pack_lanes(tiles, width):
    pieces = [None] * ((len(tiles) * width + 127) // 128)
    lanes = lane_iota((4, 128))

    def put(index, value):
        pieces[index] = value if pieces[index] is None else pieces[index] + value

    for index, tile in enumerate(tiles):
        chunk, offset = divmod(index * width, 128)
        turned = pltpu.roll(tile, offset, 1) if offset else tile
        if offset + width > 128:
            put(chunk, jnp.where(lanes >= offset, turned, 0.0))
            put(chunk + 1, jnp.where(lanes < offset, turned, 0.0))
        else:
            put(chunk, turned)
    return pieces


def step_kernel(
    xs, zs, n, total,
    pos_hbm, vel_hbm, mass_hbm, tan_hbm,
    gram_ref, mat_ref, npos_ref, nvel_ref,
    pos_ref, vel_ref, mass_ref, tan_ref, in_sem,
    row_z, row_p, dx_buf, src, tgt, k_hi, k_lo, dx_b,
    ext_send, ext_recv, out_send, out_recv,
    g_own, g_plane, g_mine, g_line, g_all,
    pz_send, pz_recv, pp_send, pp_recv, ps_send, ps_recv,
    hop_send, hop_recv, sh_send, sh_recv,
    ex_send, ex_recv, rs_send, rs_recv, gs_send, gs_recv,
):
    blk, lane = lax.axis_index("blk"), lax.axis_index("lane")
    core = lax.rem(blk, 2)
    px = blk // 4
    py = lax.rem(lane, 2) * 2 + lax.rem(blk // 2, 2)
    z = lane // 2
    planes = xs * Y
    targets = planes * n
    sources = 2 * zs * n
    passes, phases = RING[zs]

    def plane_peer(i, j, other=0):
        ox, oy = lax.rem(px + i, xs), lax.rem(py + j, Y)
        there = 1 - core if other else core
        return (ox * 4 + lax.rem(oy, 2) * 2 + there, z * 2 + oy // 2), ox * Y + oy, there

    def plane_back(i, j):
        return lax.rem(xs - i, xs) * Y + lax.rem(Y - j, Y)

    def away(length, r):
        return min(r, length - r)

    line = sorted(range(1, zs), key=lambda r: -away(zs, r))
    plane = sorted(range(1, planes), key=lambda t: -away(xs, t // Y) - away(Y, t % Y))
    both = [(t, other) for t in plane for other in range(2)] + [(0, 1)]

    def line_peer(r):
        return (blk, lax.rem(z + r, zs) * 2 + lax.rem(lane, 2))

    sibling = (blk + 1 - 2 * core, lane)
    here = px * Y + py

    def remote(source, target, send_sem, recv_sem, device):
        return pltpu.make_async_remote_copy(
            src_ref=source, dst_ref=target, send_sem=send_sem, recv_sem=recv_sem,
            device_id=device, device_id_type=MESH,
        )

    loads = [
        pltpu.make_async_copy(source, target, in_sem.at[index])
        for index, (source, target) in enumerate(
            [(pos_hbm, pos_ref), (vel_hbm, vel_ref), (mass_hbm, mass_ref), (tan_hbm, tan_ref)]
        )
    ]
    for load in loads:
        load.start()
    barrier = pltpu.get_barrier_semaphore()
    for r in line:
        pl.semaphore_signal(barrier, inc=1, device_id=line_peer(r), device_id_type=MESH)
    for t, other in both:
        pl.semaphore_signal(barrier, inc=1, device_id=plane_peer(t // Y, t % Y, other)[0], device_id_type=MESH)

    for load in loads:
        load.wait()
    pos_half = pos_ref[...] + HALF * vel_ref[...]
    row_z[0, 0] = jnp.zeros((4, 128), jnp.float32)
    row_z[0, 0, 0:3, 0:n] = pos_half
    row_z[0, 0, 3:4, 0:n] = mass_ref[...] / total
    row_p[0] = row_z[0, 0]
    dx_half = tan_ref[0:3] + HALF * tan_ref[3:6]
    dx_buf[:, 0, 0] = dx_half
    pl.semaphore_wait(barrier, zs - 1 + 2 * planes - 1)

    pending = []
    for r in line:
        remote(row_z.at[0, 0], row_z.at[0, zs - r], pz_send, pz_recv, line_peer(r)).start()
    for t in plane:
        remote(row_z.at[0, 0], row_p.at[plane_back(t // Y, t % Y)], pp_send, pp_recv, plane_peer(t // Y, t % Y)[0]).start()

    line_slots, plane_slots = row_z.at[0, pl.ds(1, zs - 1)], row_p.at[pl.ds(1, planes - 1)]
    line_all = remote(line_slots, line_slots, pz_send, pz_recv, sibling)
    plane_all = remote(plane_slots, plane_slots, pp_send, pp_recv, sibling)
    pending += [line_all.wait_send, plane_all.wait_send]

    def begin(copy):
        copy.start()
        pending.append(copy.wait_send)

    def hop(start, end):
        return remote(
            dx_buf.at[:, 0, -start % zs], dx_buf.at[:, 0, -end % zs],
            hop_send.at[end % zs], hop_recv.at[end % zs], line_peer((end - start) % zs),
        )

    before = {end: start for start, ends in passes.items() for end in ends}

    def share(r):
        return remote(dx_buf.at[:, 0, r], dx_buf.at[:, 1, r], sh_send.at[r], sh_recv.at[r], sibling)

    def visit(place):
        if place:
            hop(before[place], place).wait_recv()
        for end in passes.get(place, ()):
            begin(hop(place, end))
        begin(share(-place % zs))

    visit(0)
    for place in phases[0]:
        visit(place)
    line_all.wait_recv()
    line_share = remote(row_z.at[0], row_z.at[1], ps_send, ps_recv, sibling)
    begin(line_share)
    plane_all.wait_recv()
    for c, piece in enumerate(pack_lanes([row_p[t] for t in range(planes)], n)):
        tgt[c * 128:(c + 1) * 128, 0:8] = jnp.concatenate([piece, piece], axis=0).T
    for place in phases[1]:
        visit(place)
    line_share.wait_recv()
    tiles = [row_z[h, r] for h in range(2) for r in range(zs)]
    for c, piece in enumerate(pack_lanes(tiles, n)):
        src[:, c * 128:(c + 1) * 128] = piece

    subs = 2 * n // 16
    lanes16 = lane_iota((16, 128))

    def pair_block(b, _):
        pair, sub = b // subs, lax.rem(b, subs)
        base = pair * (6 * n) + sub * 16
        place = tgt[pl.ds(pl.multiple_of(b * 16, 16), 16), 0:8]
        own = [jnp.broadcast_to(place[:, a:a + 1], (16, 128)) for a in range(3)]
        sums = [None] * 9
        for c in range(sources // 128):
            columns = pl.ds(c * 128, 128)
            d = [src[a:a + 1, columns] - own[a] for a in range(3)]
            squared = d[0] * d[0] + d[1] * d[1] + d[2] * d[2] + SOFT
            inverse = lax.rsqrt(squared)
            inverse2 = inverse * inverse
            near = src[3:4, columns] * inverse * inverse2
            tide = 3.0 * near * inverse2
            td = [tide * d[a] for a in range(3)]
            part = {}
            for a in range(3):
                for e in range(a, 3):
                    product = td[a] * d[e]
                    part[a, e] = near - product if a == e else -product
            terms = [near * d[a] for a in range(3)] + [part[a, e] for a in range(3) for e in range(a, 3)]
            sums = [t if s is None else s + t for s, t in zip(sums, terms)]
            for a in range(3):
                for e in range(a, 3):
                    high = part[a, e].astype(jnp.bfloat16)
                    low = (part[a, e] - high.astype(jnp.float32)).astype(jnp.bfloat16)
                    for f, g in {(a, e), (e, a)}:
                        where = (pl.ds(pl.multiple_of(base + f * 2 * n, 16), 16), pl.ds(g * sources + c * 128, 128))
                        k_hi[where] = high
                        k_lo[where] = low
        tile = jnp.zeros((16, 128), jnp.float32)
        for k, s in enumerate(sums):
            tile = jnp.where(lanes16 == k, jnp.sum(s, axis=1, keepdims=True), tile)
        ext_send[pl.ds(pl.multiple_of(b * 16, 16), 16), :] = tile
        return 0

    blocks = targets // 16
    most = blocks * 5 // 8
    lax.fori_loop(0, most, pair_block, 0)
    for place in phases[2]:
        visit(place)
    lax.fori_loop(most, blocks, pair_block, 0)

    for t in plane:
        back = plane_back(t // Y, t % Y)
        remote(
            ext_send.at[pl.ds(t * n, n)], ext_recv.at[back - 1], ex_send, ex_recv, plane_peer(t // Y, t % Y)[0]
        ).start()

    ext_all = remote(ext_recv, ext_recv, ex_send, ex_recv, sibling)
    pending.append(ext_all.wait_send)
    for r in range(zs):
        share(r).wait_recv()
    for b in range(3):
        for h in range(2):
            block = dx_buf[b, h].reshape(zs * n, 128)
            high = block.astype(jnp.bfloat16)
            low = (block - high.astype(jnp.float32)).astype(jnp.bfloat16)
            start = b * sources + h * zs * n
            dx_b[start:start + zs * n, 0:128] = high
            dx_b[start:start + zs * n, 128:256] = low

    group = 4
    rows = group * 3 * n

    def pull_group(step, _):
        g = jnp.where(step < 2, step + 2, 3 - step) if xs == 4 else step
        where = pl.ds(pl.multiple_of(g * rows, 16), rows)
        first = jnp.dot(k_hi[where, :], dx_b[...], preferred_element_type=jnp.float32)
        second = jnp.dot(k_lo[where, :], dx_b[:, 0:128], preferred_element_type=jnp.float32)
        pulled = first[:, 0:128] + (first[:, 128:256] + second)
        out_send[pl.ds(g * (group // 2), group // 2)] = pulled.reshape(group // 2, 3, 2, n, 128)
        for u in (2, 1, 3, 0):
            t = g * group + u
            i, j = t // Y, lax.rem(t, Y)

            @pl.when(t != 0)
            def _():
                remote(
                    out_send.at[t // 2, :, lax.rem(t, 2)], out_recv.at[plane_back(i, j) - 1],
                    rs_send, rs_recv, plane_peer(i, j)[0],
                ).start()

        return 0

    lax.fori_loop(0, planes // group, pull_group, 0)

    out_all = remote(out_recv, out_recv, rs_send, rs_recv, sibling)
    pending.append(out_all.wait_send)
    ext_all.wait_recv()
    extra = ext_send[0:n, :]
    for t in range(planes - 1):
        extra = extra + ext_recv[t]
    acceleration = extra.T[0:3, :]
    new_velocities = vel_ref[...] + STEP * acceleration
    nvel_ref[...] = new_velocities
    npos_ref[...] = pos_half + HALF * new_velocities
    index = {}
    for a in range(3):
        for e in range(a, 3):
            index[a, e] = index[e, a] = 3 + len(set(index.values()))
    offset = []
    for a in range(3):
        taken = 0.0
        for e in range(3):
            taken = taken + extra[:, index[a, e]:index[a, e] + 1] * dx_buf[e, 0, 0]
        offset.append(taken)

    out_all.wait_recv()
    for a in range(3):
        pulled = out_send[0, a, 0]
        for t in range(planes - 1):
            pulled = pulled + out_recv[t, a]
        dv_new = tan_ref[3 + a] + STEP * (pulled - offset[a])
        mat_ref[3 + a] = dv_new
        mat_ref[a] = dx_buf[a, 0, 0] + HALF * dv_new
    matrix = mat_ref[...].reshape(6 * n, 128)
    gram = lax.dot_general(
        matrix, matrix, (((0,), (0,)), ((), ())), precision=HIGHEST, preferred_element_type=jnp.float32
    )

    part_rows = 64 // planes
    g_own[...] = gram.reshape(2 * planes, part_rows, 128)
    for t, other in both:
        device, place, there = plane_peer(t // Y, t % Y, other)
        remote(
            g_own.at[there * planes + place], g_plane.at[plane_back(t // Y, t % Y) * 2 + other - 1],
            gs_send.at[0], gs_recv.at[0], device,
        ).start()
    plane_sums = remote(g_plane, g_plane, gs_send.at[0], gs_recv.at[0], sibling)
    pending.append(plane_sums.wait_send)
    plane_sums.wait_recv()
    own = core * planes + here
    mine = g_own[own]
    for t in range(2 * planes - 1):
        mine = mine + g_plane[t]
    g_mine[...] = mine
    for r in line:
        remote(g_mine, g_line.at[zs - r - 1], gs_send.at[1], gs_recv.at[1], line_peer(r)).start()
    line_sums = remote(g_line, g_line, gs_send.at[1], gs_recv.at[1], sibling)
    pending.append(line_sums.wait_send)
    line_sums.wait_recv()
    for r in range(zs - 1):
        mine = mine + g_line[r]
    g_all[own] = mine / (6.0 * total)
    for t, other in both:
        remote(
            g_all.at[own], g_all.at[own], gs_send.at[2], gs_recv.at[2], plane_peer(t // Y, t % Y, other)[0]
        ).start()
    whole = g_all.at[pl.ds(0, 2 * planes - 1)]
    whole = remote(whole, whole, gs_send.at[2], gs_recv.at[2], sibling)
    pending.append(whole.wait_send)
    whole.wait_recv()
    gram_ref[...] = g_all[...].reshape(128, 128)

    for wait in pending:
        wait()


def factor_kernel(gram_ref, mat_ref, npos_ref, nvel_ref, pos_out, vel_out, basis_out, growth_out):
    k = gram_ref.shape[0]
    count = k // 8
    pos_out[...] = npos_ref[...]
    vel_out[...] = nvel_ref[...]
    lanes = lane_iota((8, k))
    rows = lax.broadcasted_iota(jnp.int32, (8, k), 0)
    a = [gram_ref[8 * i:8 * i + 8, :] for i in range(count)]
    q = [jnp.where(lanes == rows + 8 * i, 1.0, 0.0) for i in range(count)]
    full = lambda row: jnp.broadcast_to(row, (8, k))
    inverse_rows = []
    for b in range(count):
        c = {
            i: [jnp.broadcast_to(a[i][:, 8 * b + e:8 * b + e + 1], (8, k)) for e in range(8)]
            for i in range(b, count)
        }
        scale = jnp.ones((8, k), jnp.float32)
        for r in range(8):
            arow, qrow = full(a[b][r:r + 1, :]), full(q[b][r:r + 1, :])
            crow = {e: full(c[b][e][r:r + 1, :]) for e in range(r, 8)}
            scale = jnp.where(rows == r, lax.rsqrt(crow[r]), scale)
            inverse = 1.0 / crow[r]
            for i in range(b, count):
                m = c[i][r] * inverse
                if i == b:
                    m = jnp.where(rows > r, m, 0.0)
                a[i] = a[i] - m * arow
                q[i] = q[i] - m * qrow
                for e in range(r + 1, 8):
                    c[i][e] = c[i][e] - m * crow[e]
        growth_out[8 * b:8 * b + 8, :] = jnp.where(lanes >= rows + 8 * b, a[b] * scale, 0.0)
        inverse_rows.append(q[b] * scale)
    inverse = jnp.concatenate(inverse_rows, axis=0)
    matrix = mat_ref[...].reshape(-1, k)
    basis = lax.dot_general(
        matrix, inverse, (((1,), (1,)), ((), ())), precision=HIGHEST, preferred_element_type=jnp.float32
    )
    basis_out[...] = basis.reshape(basis_out.shape)


def body(positions, velocities, masses, tangents):
    n, k = positions.shape[1], tangents.shape[2]
    xs, zs = lax.axis_size("blk") // 4, lax.axis_size("lane") // 2
    planes = xs * Y
    total = float(n * planes * zs * 2)
    targets, sources = planes * n, 2 * zs * n
    f32, bf16 = jnp.float32, jnp.bfloat16
    vmem = pl.BlockSpec(memory_space=pltpu.VMEM)
    dma = pltpu.SemaphoreType.DMA
    part_rows = 64 // planes
    scratch = [
        pltpu.VMEM((3, n), f32),
        pltpu.VMEM((3, n), f32),
        pltpu.VMEM((1, n), f32),
        pltpu.VMEM((6, n, k), f32),
        dma((4,)),
        pltpu.VMEM((2, zs, 4, 128), f32),
        pltpu.VMEM((planes, 4, 128), f32),
        pltpu.VMEM((3, 2, zs, n, k), f32),
        pltpu.VMEM((4, sources), f32),
        pltpu.VMEM(((targets + 127) // 128 * 128, 128), f32),
        pltpu.VMEM((3 * targets, 3 * sources), bf16),
        pltpu.VMEM((3 * targets, 3 * sources), bf16),
        pltpu.VMEM((3 * sources, 2 * k), bf16),
        pltpu.VMEM((targets, 128), f32),
        pltpu.VMEM((planes - 1, n, 128), f32),
        pltpu.VMEM((planes // 2, 3, 2, n, k), f32),
        pltpu.VMEM((planes - 1, 3, n, k), f32),
        pltpu.VMEM((2 * planes, part_rows, k), f32),
        pltpu.VMEM((2 * planes - 1, part_rows, k), f32),
        pltpu.VMEM((part_rows, k), f32),
        pltpu.VMEM((zs - 1, part_rows, k), f32),
        pltpu.VMEM((2 * planes, part_rows, k), f32),
        dma, dma, dma, dma, dma, dma,
        dma((zs,)), dma((zs,)),
        dma((zs,)), dma((zs,)),
        dma, dma, dma, dma, dma((3,)), dma((3,)),
    ]
    gram, matrix, npos, nvel = pl.pallas_call(
        functools.partial(step_kernel, xs, zs, n, total),
        out_shape=[
            jax.ShapeDtypeStruct((k, k), f32),
            jax.ShapeDtypeStruct((6, n, k), f32),
            jax.ShapeDtypeStruct((3, n), f32),
            jax.ShapeDtypeStruct((3, n), f32),
        ],
        in_specs=[pl.BlockSpec(memory_space=pltpu.HBM)] * 4,
        out_specs=[vmem] * 4,
        scratch_shapes=scratch,
        compiler_params=pltpu.CompilerParams(
            collective_id=0, has_side_effects=True, vmem_limit_bytes=40 * 1024 * 1024
        ),
    )(*[
        pltpu.with_memory_space_constraint(array, pltpu.HBM)
        for array in (positions, velocities, masses.reshape(1, n), tangents)
    ])
    npos, nvel, basis, growth = pl.pallas_call(
        factor_kernel,
        out_shape=[
            jax.ShapeDtypeStruct((3, n), f32),
            jax.ShapeDtypeStruct((3, n), f32),
            jax.ShapeDtypeStruct((6, n, k), f32),
            jax.ShapeDtypeStruct((k, k), f32),
        ],
        in_specs=[vmem] * 4,
        out_specs=[vmem] * 4,
        compiler_params=pltpu.CompilerParams(vmem_limit_bytes=40 * 1024 * 1024),
    )(gram, matrix, npos, nvel)
    return (npos, nvel, basis, growth)


def solution(mesh):
    return jax.shard_map(
        body,
        mesh=mesh,
        in_specs=(
            P(None, ("blk", "lane")),
            P(None, ("blk", "lane")),
            P(("blk", "lane")),
            P(None, ("blk", "lane"), None),
        ),
        out_specs=(
            P(None, ("blk", "lane")),
            P(None, ("blk", "lane")),
            P(None, ("blk", "lane"), None),
            P(),
        ),
        check_vma=False,
    )
```

```python
import functools

import jax
import jax.numpy as jnp
from jax import lax
from jax.experimental import pallas as pl
from jax.experimental.pallas import tpu as pltpu
from jax.sharding import PartitionSpec as P

STEP = 0.0625
SOFT = 0.0025
HALF = 0.5 * STEP
MESH = pl.DeviceIdType.MESH
HIGHEST = lax.Precision.HIGHEST
Y = 4


RING = {
    16: (
        {0: (3, -3, 1, -1), 3: (6, 2, 4), -3: (-6, -2, -4), 6: (8, 5, 7), -6: (-5, -7)},
        ((0, 3, -3, 1, -1), (6, -6, 2, -2, 4, -4), (5, -5, 7, -7, 8)),
        3,
    ),
    4: ({0: (1, -1), 1: (2,)}, ((0, 1), (-1,), (2,)), 1),
}


def lane_iota(shape):
    return lax.broadcasted_iota(jnp.int32, shape, 1)


def pack_lanes(tile_of, count, width, chunk):
    lanes = lane_iota((4, 128))
    total = jnp.zeros((4, 128), jnp.float32)
    for index in range(128 * chunk // width, min(count, (128 * chunk + 127) // width + 1)):
        first, offset = divmod(index * width, 128)
        turned = pltpu.roll(tile_of(index), offset, 1) if offset else tile_of(index)
        if offset + width > 128:
            turned = jnp.where((lanes >= offset) if first == chunk else (lanes < offset), turned, 0.0)
        total = total + turned
    return total


def step_kernel(
    xs, zs, n, total,
    pos_hbm, vel_hbm, mass_hbm, tan_hbm,
    gram_ref, mat_ref, npos_ref, nvel_ref,
    pos_ref, vel_ref, mass_ref, tan_ref, in_sem,
    row_p, dx_buf, src, tgt, k_hi, k_lo, dx_b,
    ext_all_rows, ext_send, ext_recv, out_send, out_recv,
    g_own, g_plane, g_mine, g_line, g_all,
    pp_send, pp_recv,
    hop_send, hop_recv, sh_send, sh_recv,
    ex_send, ex_recv, rs_send, rs_recv, gs_send, gs_recv,
):
    blk, lane = lax.axis_index("blk"), lax.axis_index("lane")
    core = lax.rem(blk, 2)
    px = blk // 4
    py = lax.rem(lane, 2) * 2 + lax.rem(blk // 2, 2)
    z = lane // 2
    planes = xs * Y
    targets = planes * n
    sources = 2 * zs * n
    passes, phases, reach = RING[zs]
    order = [(h, place) for group in phases for h in range(2) for place in group]
    early = 2 * (len(phases[0]) + len(phases[1])) * n // 128
    split = 3 * 128 * early
    width = sources // 128 - early

    def column(b, chunk):
        return 128 * (b * early + chunk) if chunk < early else split + 128 * (b * width + chunk - early)

    def plane_peer(i, j, other=0):
        ox, oy = lax.rem(px + i, xs), lax.rem(py + j, Y)
        there = 1 - core if other else core
        return (ox * 4 + lax.rem(oy, 2) * 2 + there, z * 2 + oy // 2), ox * Y + oy, there

    def plane_back(i, j):
        return lax.rem(xs - i, xs) * Y + lax.rem(Y - j, Y)

    def away(length, r):
        return min(r, length - r)

    line = sorted(range(1, zs), key=lambda r: -away(zs, r))
    plane = sorted(range(1, planes), key=lambda t: -away(xs, t // Y) - away(Y, t % Y))
    both = [(t, other) for t in plane for other in range(2)] + [(0, 1)]

    def line_peer(r):
        return (blk, lax.rem(z + r, zs) * 2 + lax.rem(lane, 2))

    sibling = (blk + 1 - 2 * core, lane)
    here = px * Y + py

    def remote(source, target, send_sem, recv_sem, device):
        return pltpu.make_async_remote_copy(
            src_ref=source, dst_ref=target, send_sem=send_sem, recv_sem=recv_sem,
            device_id=device, device_id_type=MESH,
        )

    loads = [
        pltpu.make_async_copy(source, target, in_sem.at[index])
        for index, (source, target) in enumerate(
            [(pos_hbm, pos_ref), (vel_hbm, vel_ref), (mass_hbm, mass_ref), (tan_hbm, tan_ref)]
        )
    ]
    for load in loads:
        load.start()
    barrier = pltpu.get_barrier_semaphore()
    near = sorted({r % zs for r in range(-reach, reach + 1)} - {0}, key=lambda r: -away(zs, r))
    for r in near:
        pl.semaphore_signal(barrier, inc=1, device_id=line_peer(r), device_id_type=MESH)
    for t in plane:
        pl.semaphore_signal(barrier, inc=1, device_id=plane_peer(t // Y, t % Y)[0], device_id_type=MESH)
    pl.semaphore_signal(barrier, inc=1, device_id=sibling, device_id_type=MESH)

    for load in loads:
        load.wait()
    pos_half = pos_ref[...] + HALF * vel_ref[...]
    row_p[0] = jnp.zeros((4, 128), jnp.float32)
    row_p[0, 0:3, 0:n] = pos_half
    row_p[0, 3:4, 0:n] = mass_ref[...] / total
    dx_half = tan_ref[0:3] + HALF * tan_ref[3:6]
    dx_buf[0, 0, 0:3 * n] = dx_half.reshape(3 * n, 128)
    dx_buf[0, 0, 3 * n:3 * n + 4] = row_p[0]
    dx_buf[0, 0, 3 * n + 4:3 * n + 8] = jnp.zeros((4, 128), jnp.float32)
    pl.semaphore_wait(barrier, len(near) + planes)

    pending = []
    plane_slots = row_p.at[pl.ds(1, planes - 1)]
    plane_all = remote(plane_slots, plane_slots, pp_send, pp_recv, sibling)

    def begin(copy):
        copy.start()
        pending.append(copy.wait_send)

    def hop(start, end):
        return remote(
            dx_buf.at[0, -start % zs], dx_buf.at[0, -end % zs],
            hop_send.at[end % zs], hop_recv.at[end % zs], line_peer((end - start) % zs),
        )

    before = {end: start for start, ends in passes.items() for end in ends}

    def share(r):
        return remote(dx_buf.at[0, r], dx_buf.at[1, r], sh_send.at[r], sh_recv.at[r], sibling)

    def visit(place):
        if place:
            hop(before[place], place).wait_recv()
        for end in passes.get(place, ()):
            begin(hop(place, end))
        begin(share(-place % zs))

    def joined(group):
        for place in group:
            share(-place % zs).wait_recv()

    def pack_sources(chunks):
        def tile_of(q):
            h, place = order[q]
            return dx_buf[h, -place % zs, 3 * n:3 * n + 4, :]

        for chunk in chunks:
            src[:, 128 * chunk:128 * chunk + 128] = pack_lanes(tile_of, 2 * zs, n, chunk)

    visit(0)
    for t in plane:
        remote(row_p.at[0], row_p.at[plane_back(t // Y, t % Y)], pp_send, pp_recv, plane_peer(t // Y, t % Y)[0]).start()
    pending.append(plane_all.wait_send)
    for place in phases[0][1:]:
        visit(place)
    plane_all.wait_recv()
    for c in range((targets + 127) // 128):
        piece = pack_lanes(lambda t: row_p[t], planes, n, c)
        tgt[c * 128:(c + 1) * 128, 0:8] = jnp.concatenate([piece, piece], axis=0).T
    subs = 2 * n // 16
    lanes16 = lane_iota((16, 128))

    def pair_block(chunks, b, _):
        pair, sub = b // subs, lax.rem(b, subs)
        base = pair * (6 * n) + sub * 16
        place = tgt[pl.ds(pl.multiple_of(b * 16, 16), 16), 0:8]
        own = [jnp.broadcast_to(place[:, a:a + 1], (16, 128)) for a in range(3)]
        sums = [None] * 9
        for c in chunks:
            columns = pl.ds(c * 128, 128)
            d = [src[a:a + 1, columns] - own[a] for a in range(3)]
            squared = d[0] * d[0] + d[1] * d[1] + d[2] * d[2] + SOFT
            inverse = lax.rsqrt(squared)
            inverse2 = inverse * inverse
            near = src[3:4, columns] * inverse * inverse2
            tide = 3.0 * near * inverse2
            td = [tide * d[a] for a in range(3)]
            part = {}
            for a in range(3):
                for e in range(a, 3):
                    product = td[a] * d[e]
                    part[a, e] = near - product if a == e else -product
            terms = [near * d[a] for a in range(3)] + [part[a, e] for a in range(3) for e in range(a, 3)]
            sums = [t if s is None else s + t for s, t in zip(sums, terms)]
            for a in range(3):
                for e in range(a, 3):
                    high = part[a, e].astype(jnp.bfloat16)
                    low = (part[a, e] - high.astype(jnp.float32)).astype(jnp.bfloat16)
                    for f, g in {(a, e), (e, a)}:
                        where = (pl.ds(pl.multiple_of(base + f * 2 * n, 16), 16), pl.ds(column(g, c), 128))
                        k_hi[where] = high
                        k_lo[where] = low
        tile = jnp.zeros((16, 128), jnp.float32)
        for k, s in enumerate(sums):
            tile = jnp.where(lanes16 == k, jnp.sum(s, axis=1, keepdims=True), tile)
        where = pl.ds(pl.multiple_of(b * 16, 16), 16)
        ext_all_rows[where, :] = tile if chunks[0] == 0 else ext_all_rows[where, :] + tile
        return 0

    progress = [0, 0]

    def take(count):
        chunks = range(progress[0], count * n // 128)
        if len(chunks):
            progress[0] = chunks[-1] + 1
            pack_sources(chunks)
            lax.fori_loop(0, targets // 16, functools.partial(pair_block, list(chunks)), 0)

    def halves(count):
        for q in range(progress[1], count, 2):
            for b in range(3):
                block = jnp.concatenate(
                    [dx_buf[h, -place % zs, b * n:(b + 1) * n, :] for h, place in order[q:q + 2]], axis=0
                )
                first = q * n
                while first < (q + 2) * n:
                    last = min((q + 2) * n, first // 128 * 128 + 128)
                    part = block[first - q * n:last - q * n, :]
                    high = part.astype(jnp.bfloat16)
                    low = (part - high.astype(jnp.float32)).astype(jnp.bfloat16)
                    start = column(b, first // 128) + first % 128
                    dx_b[start:start + last - first, 0:128] = high
                    dx_b[start:start + last - first, 128:256] = low
                    first = last
        progress[1] = count

    group = 4
    rows = group * 3 * n

    def pull(g, low, high):
        where = pl.ds(pl.multiple_of(g * rows, 16), rows)
        first = jnp.dot(k_hi[where, low:high], dx_b[low:high, :], preferred_element_type=jnp.float32)
        second = jnp.dot(k_lo[where, low:high], dx_b[low:high, 0:128], preferred_element_type=jnp.float32)
        pulled = first[:, 0:128] + (first[:, 128:256] + second)
        return pulled.reshape(group // 2, 3, 2, n, 128)

    def early_group(g, _):
        out_send[pl.ds(g * (group // 2), group // 2)] = pull(g, 0, split)
        return 0

    joined(phases[0])
    count = 2 * len(phases[0])
    take(count)
    for place in phases[1]:
        visit(place)
    joined(phases[1])
    count += 2 * len(phases[1])
    take(count)
    for place in phases[2]:
        visit(place)
    halves(count)
    if early:
        lax.fori_loop(0, planes // group, early_group, 0)
    take(count + len(phases[2]))
    joined(phases[2])
    take(2 * zs)

    for t in range(planes):
        tile = ext_all_rows[t * n:t * n + 8, :]
        for u in range(1, n // 8):
            tile = tile + pltpu.roll(ext_all_rows[t * n + 8 * u:t * n + 8 * u + 8, :], 16 * u, 1)
        ext_send[t] = tile
    for t in plane:
        back = plane_back(t // Y, t % Y)
        remote(
            ext_send.at[t], ext_recv.at[back - 1], ex_send, ex_recv, plane_peer(t // Y, t % Y)[0]
        ).start()

    ext_all = remote(ext_recv, ext_recv, ex_send, ex_recv, sibling)
    pending.append(ext_all.wait_send)
    halves(2 * zs)

    def pull_group(step, _):
        g = jnp.where(step < 2, step + 2, 3 - step) if xs == 4 else step
        half = pl.ds(g * (group // 2), group // 2)
        pulled = pull(g, split, 3 * sources)
        out_send[half] = out_send[half] + pulled if early else pulled
        for u in (2, 1, 3, 0):
            t = g * group + u
            i, j = t // Y, lax.rem(t, Y)

            @pl.when(t != 0)
            def _():
                remote(
                    out_send.at[t // 2, :, lax.rem(t, 2)], out_recv.at[plane_back(i, j) - 1],
                    rs_send, rs_recv, plane_peer(i, j)[0],
                ).start()

        return 0

    lax.fori_loop(0, planes // group, pull_group, 0)

    out_all = remote(out_recv, out_recv, rs_send, rs_recv, sibling)
    pending.append(out_all.wait_send)
    ext_all.wait_recv()
    extra = ext_send[0]
    for t in range(planes - 1):
        extra = extra + ext_recv[t]
    extra = jnp.concatenate(
        [pltpu.roll(extra, 128 - 16 * u, 1) if u else extra for u in range(n // 8)], axis=0
    )
    acceleration = extra.T[0:3, :]
    new_velocities = vel_ref[...] + STEP * acceleration
    nvel_ref[...] = new_velocities
    npos_ref[...] = pos_half + HALF * new_velocities
    index = {}
    for a in range(3):
        for e in range(a, 3):
            index[a, e] = index[e, a] = 3 + len(set(index.values()))
    offset = []
    for a in range(3):
        taken = 0.0
        for e in range(3):
            taken = taken + extra[:, index[a, e]:index[a, e] + 1] * dx_buf[0, 0, e * n:(e + 1) * n, :]
        offset.append(taken)

    out_all.wait_recv()
    for a in range(3):
        pulled = out_send[0, a, 0]
        for t in range(planes - 1):
            pulled = pulled + out_recv[t, a]
        dv_new = tan_ref[3 + a] + STEP * (pulled - offset[a])
        mat_ref[3 + a] = dv_new
        mat_ref[a] = dx_buf[0, 0, a * n:(a + 1) * n, :] + HALF * dv_new
    matrix = mat_ref[...].reshape(6 * n, 128)
    gram = lax.dot_general(
        matrix, matrix, (((0,), (0,)), ((), ())), precision=HIGHEST, preferred_element_type=jnp.float32
    )

    part_rows = 64 // planes
    g_own[...] = gram.reshape(2 * planes, part_rows, 128)
    for t, other in both:
        device, place, there = plane_peer(t // Y, t % Y, other)
        remote(
            g_own.at[there * planes + place], g_plane.at[plane_back(t // Y, t % Y) * 2 + other - 1],
            gs_send.at[0], gs_recv.at[0], device,
        ).start()
    plane_sums = remote(g_plane, g_plane, gs_send.at[0], gs_recv.at[0], sibling)
    pending.append(plane_sums.wait_send)
    plane_sums.wait_recv()
    own = core * planes + here
    mine = g_own[own]
    for t in range(2 * planes - 1):
        mine = mine + g_plane[t]
    g_mine[...] = mine
    for r in line:
        remote(g_mine, g_line.at[zs - r - 1], gs_send.at[1], gs_recv.at[1], line_peer(r)).start()
    line_sums = remote(g_line, g_line, gs_send.at[1], gs_recv.at[1], sibling)
    pending.append(line_sums.wait_send)
    line_sums.wait_recv()
    for r in range(zs - 1):
        mine = mine + g_line[r]
    g_all[own] = mine / (6.0 * total)
    for t, other in both:
        remote(
            g_all.at[own], g_all.at[own], gs_send.at[2], gs_recv.at[2], plane_peer(t // Y, t % Y, other)[0]
        ).start()
    whole = g_all.at[pl.ds(0, 2 * planes - 1)]
    whole = remote(whole, whole, gs_send.at[2], gs_recv.at[2], sibling)
    pending.append(whole.wait_send)
    whole.wait_recv()
    gram_ref[...] = g_all[...].reshape(128, 128)

    for wait in pending:
        wait()


def factor_kernel(gram_ref, mat_ref, npos_ref, nvel_ref, pos_out, vel_out, basis_out, growth_out):
    k = gram_ref.shape[0]
    count = k // 8
    pos_out[...] = npos_ref[...]
    vel_out[...] = nvel_ref[...]
    lanes = lane_iota((8, k))
    rows = lax.broadcasted_iota(jnp.int32, (8, k), 0)
    a = [gram_ref[8 * i:8 * i + 8, :] for i in range(count)]
    q = [jnp.where(lanes == rows + 8 * i, 1.0, 0.0) for i in range(count)]
    full = lambda row: jnp.broadcast_to(row, (8, k))
    inverse_rows = []
    for b in range(count):
        c = {
            i: [jnp.broadcast_to(a[i][:, 8 * b + e:8 * b + e + 1], (8, k)) for e in range(8)]
            for i in range(b, count)
        }
        scale = jnp.ones((8, k), jnp.float32)
        for r in range(8):
            arow, qrow = full(a[b][r:r + 1, :]), full(q[b][r:r + 1, :])
            crow = {e: full(c[b][e][r:r + 1, :]) for e in range(r, 8)}
            scale = jnp.where(rows == r, lax.rsqrt(crow[r]), scale)
            inverse = 1.0 / crow[r]
            for i in range(b, count):
                m = c[i][r] * inverse
                if i == b:
                    m = jnp.where(rows > r, m, 0.0)
                a[i] = a[i] - m * arow
                q[i] = q[i] - m * qrow
                for e in range(r + 1, 8):
                    c[i][e] = c[i][e] - m * crow[e]
        growth_out[8 * b:8 * b + 8, :] = jnp.where(lanes >= rows + 8 * b, a[b] * scale, 0.0)
        inverse_rows.append(q[b] * scale)
    inverse = jnp.concatenate(inverse_rows, axis=0)
    matrix = mat_ref[...].reshape(-1, k)
    basis = lax.dot_general(
        matrix, inverse, (((1,), (1,)), ((), ())), precision=HIGHEST, preferred_element_type=jnp.float32
    )
    basis_out[...] = basis.reshape(basis_out.shape)


def body(positions, velocities, masses, tangents):
    n, k = positions.shape[1], tangents.shape[2]
    xs, zs = lax.axis_size("blk") // 4, lax.axis_size("lane") // 2
    planes = xs * Y
    total = float(n * planes * zs * 2)
    targets, sources = planes * n, 2 * zs * n
    f32, bf16 = jnp.float32, jnp.bfloat16
    vmem = pl.BlockSpec(memory_space=pltpu.VMEM)
    dma = pltpu.SemaphoreType.DMA
    part_rows = 64 // planes
    scratch = [
        pltpu.VMEM((3, n), f32),
        pltpu.VMEM((3, n), f32),
        pltpu.VMEM((1, n), f32),
        pltpu.VMEM((6, n, k), f32),
        dma((4,)),
        pltpu.VMEM((planes, 4, 128), f32),
        pltpu.VMEM((2, zs, 3 * n + 8, k), f32),
        pltpu.VMEM((4, sources), f32),
        pltpu.VMEM(((targets + 127) // 128 * 128, 128), f32),
        pltpu.VMEM((3 * targets, 3 * sources), bf16),
        pltpu.VMEM((3 * targets, 3 * sources), bf16),
        pltpu.VMEM((3 * sources, 2 * k), bf16),
        pltpu.VMEM((targets, 128), f32),
        pltpu.VMEM((planes, 8, 128), f32),
        pltpu.VMEM((planes - 1, 8, 128), f32),
        pltpu.VMEM((planes // 2, 3, 2, n, k), f32),
        pltpu.VMEM((planes - 1, 3, n, k), f32),
        pltpu.VMEM((2 * planes, part_rows, k), f32),
        pltpu.VMEM((2 * planes - 1, part_rows, k), f32),
        pltpu.VMEM((part_rows, k), f32),
        pltpu.VMEM((zs - 1, part_rows, k), f32),
        pltpu.VMEM((2 * planes, part_rows, k), f32),
        dma, dma,
        dma((zs,)), dma((zs,)),
        dma((zs,)), dma((zs,)),
        dma, dma, dma, dma, dma((3,)), dma((3,)),
    ]
    gram, matrix, npos, nvel = pl.pallas_call(
        functools.partial(step_kernel, xs, zs, n, total),
        out_shape=[
            jax.ShapeDtypeStruct((k, k), f32),
            jax.ShapeDtypeStruct((6, n, k), f32),
            jax.ShapeDtypeStruct((3, n), f32),
            jax.ShapeDtypeStruct((3, n), f32),
        ],
        in_specs=[pl.BlockSpec(memory_space=pltpu.HBM)] * 4,
        out_specs=[vmem] * 4,
        scratch_shapes=scratch,
        compiler_params=pltpu.CompilerParams(
            collective_id=0, has_side_effects=True, vmem_limit_bytes=40 * 1024 * 1024
        ),
    )(*[
        pltpu.with_memory_space_constraint(array, pltpu.HBM)
        for array in (positions, velocities, masses.reshape(1, n), tangents)
    ])
    npos, nvel, basis, growth = pl.pallas_call(
        factor_kernel,
        out_shape=[
            jax.ShapeDtypeStruct((3, n), f32),
            jax.ShapeDtypeStruct((3, n), f32),
            jax.ShapeDtypeStruct((6, n, k), f32),
            jax.ShapeDtypeStruct((k, k), f32),
        ],
        in_specs=[vmem] * 4,
        out_specs=[vmem] * 4,
        compiler_params=pltpu.CompilerParams(vmem_limit_bytes=40 * 1024 * 1024),
    )(gram, matrix, npos, nvel)
    return (npos, nvel, basis, growth)


def solution(mesh):
    return jax.shard_map(
        body,
        mesh=mesh,
        in_specs=(
            P(None, ("blk", "lane")),
            P(None, ("blk", "lane")),
            P(("blk", "lane")),
            P(None, ("blk", "lane"), None),
        ),
        out_specs=(
            P(None, ("blk", "lane")),
            P(None, ("blk", "lane")),
            P(None, ("blk", "lane"), None),
            P(),
        ),
        check_vma=False,
    )
```

```python
import functools

import jax
import jax.numpy as jnp
from jax import lax
from jax.experimental import pallas as pl
from jax.experimental.pallas import tpu as pltpu
from jax.sharding import PartitionSpec as P

STEP = 0.0625
SOFT = 0.0025
HALF = 0.5 * STEP
MESH = pl.DeviceIdType.MESH
HIGHEST = lax.Precision.HIGHEST
Y = 4


RING = {
    16: (
        {0: (3, -3, 1, -1), 3: (6, 2, 4), -3: (-6, -2, -4), 6: (8, 5, 7), -6: (-5, -7)},
        ((0, 3, -3, 1, -1), (6, -6, 2, -2, 4, -4), (5, -5, 7, -7, 8)),
        3,
    ),
    4: ({0: (1, -1), 1: (2,)}, ((0, 1), (-1,), (2,)), 1),
}


def lane_iota(shape):
    return lax.broadcasted_iota(jnp.int32, shape, 1)


def pack_lanes(tile_of, count, width, chunk):
    lanes = lane_iota((4, 128))
    total = jnp.zeros((4, 128), jnp.float32)
    for index in range(128 * chunk // width, min(count, (128 * chunk + 127) // width + 1)):
        first, offset = divmod(index * width, 128)
        turned = pltpu.roll(tile_of(index), offset, 1) if offset else tile_of(index)
        if offset + width > 128:
            turned = jnp.where((lanes >= offset) if first == chunk else (lanes < offset), turned, 0.0)
        total = total + turned
    return total


def step_kernel(
    xs, zs, n, total,
    pos_hbm, vel_hbm, mass_hbm, tan_hbm,
    gram_ref, mat_ref, npos_ref, nvel_ref,
    pos_ref, vel_ref, mass_ref, tan_ref, in_sem,
    row_p, dx_buf, src, tgt, k_hi, k_lo, dx_b,
    lane_sums, ext_send, ext_recv, out_send, out_recv,
    g_own, g_plane, g_mine, g_line, g_all,
    pp_send, pp_recv,
    hop_send, hop_recv, sh_send, sh_recv,
    ex_send, ex_recv, rs_send, rs_recv, gs_send, gs_recv,
):
    blk, lane = lax.axis_index("blk"), lax.axis_index("lane")
    core = lax.rem(blk, 2)
    px = blk // 4
    py = lax.rem(lane, 2) * 2 + lax.rem(blk // 2, 2)
    z = lane // 2
    planes = xs * Y
    targets = planes * n
    sources = 2 * zs * n
    passes, phases, reach = RING[zs]
    order = [(h, place) for group in phases for h in range(2) for place in group]
    early = 2 * (len(phases[0]) + len(phases[1])) * n // 128
    split = 3 * 128 * early
    width = sources // 128 - early

    def column(b, chunk):
        return 128 * (b * early + chunk) if chunk < early else split + 128 * (b * width + chunk - early)

    def plane_peer(i, j, other=0):
        ox, oy = lax.rem(px + i, xs), lax.rem(py + j, Y)
        there = 1 - core if other else core
        return (ox * 4 + lax.rem(oy, 2) * 2 + there, z * 2 + oy // 2), ox * Y + oy, there

    def plane_back(i, j):
        return lax.rem(xs - i, xs) * Y + lax.rem(Y - j, Y)

    def away(length, r):
        return min(r, length - r)

    line = sorted(range(1, zs), key=lambda r: -away(zs, r))
    plane = sorted(range(1, planes), key=lambda t: -away(xs, t // Y) - away(Y, t % Y))
    both = [(t, other) for t in plane for other in range(2)] + [(0, 1)]

    def line_peer(r):
        return (blk, lax.rem(z + r, zs) * 2 + lax.rem(lane, 2))

    sibling = (blk + 1 - 2 * core, lane)
    here = px * Y + py

    def remote(source, target, send_sem, recv_sem, device):
        return pltpu.make_async_remote_copy(
            src_ref=source, dst_ref=target, send_sem=send_sem, recv_sem=recv_sem,
            device_id=device, device_id_type=MESH,
        )

    loads = [
        pltpu.make_async_copy(source, target, in_sem.at[index])
        for index, (source, target) in enumerate(
            [(pos_hbm, pos_ref), (vel_hbm, vel_ref), (mass_hbm, mass_ref), (tan_hbm, tan_ref)]
        )
    ]
    for load in loads:
        load.start()
    barrier = pltpu.get_barrier_semaphore()
    near = sorted({r % zs for r in range(-reach, reach + 1)} - {0}, key=lambda r: -away(zs, r))
    for r in near:
        pl.semaphore_signal(barrier, inc=1, device_id=line_peer(r), device_id_type=MESH)
    for t in plane:
        pl.semaphore_signal(barrier, inc=1, device_id=plane_peer(t // Y, t % Y)[0], device_id_type=MESH)
    pl.semaphore_signal(barrier, inc=1, device_id=sibling, device_id_type=MESH)

    for load in loads:
        load.wait()
    pos_half = pos_ref[...] + HALF * vel_ref[...]
    row_p[0] = jnp.zeros((4, 128), jnp.float32)
    row_p[0, 0:3, 0:n] = pos_half
    row_p[0, 3:4, 0:n] = mass_ref[...] / total
    dx_half = tan_ref[0:3] + HALF * tan_ref[3:6]
    dx_buf[0, 0, 0:3 * n] = dx_half.reshape(3 * n, 128)
    dx_buf[0, 0, 3 * n:3 * n + 4] = row_p[0]
    dx_buf[0, 0, 3 * n + 4:3 * n + 8] = jnp.zeros((4, 128), jnp.float32)
    pl.semaphore_wait(barrier, len(near) + planes)

    pending = []
    plane_slots = row_p.at[pl.ds(1, planes - 1)]
    plane_all = remote(plane_slots, plane_slots, pp_send, pp_recv, sibling)

    def begin(copy):
        copy.start()
        pending.append(copy.wait_send)

    def hop(start, end):
        return remote(
            dx_buf.at[0, -start % zs], dx_buf.at[0, -end % zs],
            hop_send.at[end % zs], hop_recv.at[end % zs], line_peer((end - start) % zs),
        )

    before = {end: start for start, ends in passes.items() for end in ends}

    def share(r):
        return remote(dx_buf.at[0, r], dx_buf.at[1, r], sh_send.at[r], sh_recv.at[r], sibling)

    def visit(place):
        if place:
            hop(before[place], place).wait_recv()
        for end in passes.get(place, ()):
            begin(hop(place, end))
        begin(share(-place % zs))

    def joined(group):
        for place in group:
            share(-place % zs).wait_recv()

    def pack_sources(chunks):
        def tile_of(q):
            h, place = order[q]
            return dx_buf[h, -place % zs, 3 * n:3 * n + 4, :]

        for chunk in chunks:
            src[:, 128 * chunk:128 * chunk + 128] = pack_lanes(tile_of, 2 * zs, n, chunk)

    visit(0)
    for t in plane:
        remote(row_p.at[0], row_p.at[plane_back(t // Y, t % Y)], pp_send, pp_recv, plane_peer(t // Y, t % Y)[0]).start()
    pending.append(plane_all.wait_send)
    for place in phases[0][1:]:
        visit(place)
    plane_all.wait_recv()
    for c in range((targets + 127) // 128):
        piece = pack_lanes(lambda t: row_p[t], planes, n, c)
        columns = jnp.concatenate([piece, piece], axis=0).T
        last = min(128, targets - c * 128)
        for a in range(3):
            tgt[a, c * 128:c * 128 + last, :] = jnp.broadcast_to(columns[0:last, a:a + 1], (last, 128))
    def pair_block(chunks, pair, _):
        where = pl.ds(pl.multiple_of(pair * 2 * n, 16), 2 * n)
        base = pair * (6 * n)
        own = [tgt[a, where, :] for a in range(3)]
        sums = [None if chunks[0] == 0 else lane_sums[k, where, :] for k in range(9)]
        for c in chunks:
            columns = pl.ds(c * 128, 128)
            d = [src[a:a + 1, columns] - own[a] for a in range(3)]
            squared = d[0] * d[0] + d[1] * d[1] + d[2] * d[2] + SOFT
            inverse = lax.rsqrt(squared)
            inverse2 = inverse * inverse
            near = src[3:4, columns] * inverse * inverse2
            tide = 3.0 * near * inverse2
            td = [tide * d[a] for a in range(3)]
            part = {}
            for a in range(3):
                for e in range(a, 3):
                    product = td[a] * d[e]
                    part[a, e] = near - product if a == e else -product
            terms = [near * d[a] for a in range(3)] + [part[a, e] for a in range(3) for e in range(a, 3)]
            sums = [t if s is None else s + t for s, t in zip(sums, terms)]
            for a in range(3):
                for e in range(a, 3):
                    high = part[a, e].astype(jnp.bfloat16)
                    low = (part[a, e] - high.astype(jnp.float32)).astype(jnp.bfloat16)
                    for f, g in {(a, e), (e, a)}:
                        to = (pl.ds(pl.multiple_of(base + f * 2 * n, 16), 2 * n), pl.ds(column(g, c), 128))
                        k_hi[to] = high
                        k_lo[to] = low
        for k in range(9):
            lane_sums[k, where, :] = sums[k]
        return 0

    progress = [0, 0]

    def take(count):
        chunks = range(progress[0], count * n // 128)
        if len(chunks):
            progress[0] = chunks[-1] + 1
            pack_sources(chunks)
            lax.fori_loop(0, planes // 2, functools.partial(pair_block, list(chunks)), 0, unroll=2)

    def halves(count):
        for q in range(progress[1], count, 2):
            for b in range(3):
                block = jnp.concatenate(
                    [dx_buf[h, -place % zs, b * n:(b + 1) * n, :] for h, place in order[q:q + 2]], axis=0
                )
                first = q * n
                while first < (q + 2) * n:
                    last = min((q + 2) * n, first // 128 * 128 + 128)
                    part = block[first - q * n:last - q * n, :]
                    high = part.astype(jnp.bfloat16)
                    low = (part - high.astype(jnp.float32)).astype(jnp.bfloat16)
                    start = column(b, first // 128) + first % 128
                    dx_b[start:start + last - first, 0:128] = high
                    dx_b[start:start + last - first, 128:256] = low
                    first = last
        progress[1] = count

    group = 4
    rows = group * 3 * n

    def pull(g, low, high):
        where = pl.ds(pl.multiple_of(g * rows, 16), rows)
        first = jnp.dot(k_hi[where, low:high], dx_b[low:high, :], preferred_element_type=jnp.float32)
        second = jnp.dot(k_lo[where, low:high], dx_b[low:high, 0:128], preferred_element_type=jnp.float32)
        pulled = first[:, 0:128] + (first[:, 128:256] + second)
        return pulled.reshape(group // 2, 3, 2, n, 128)

    def early_group(g, _):
        out_send[pl.ds(g * (group // 2), group // 2)] = pull(g, 0, split)
        return 0

    joined(phases[0])
    count = 2 * len(phases[0])
    take(count)
    for place in phases[1]:
        visit(place)
    joined(phases[1])
    count += 2 * len(phases[1])
    take(count)
    for place in phases[2]:
        visit(place)
    halves(count)
    if early:
        lax.fori_loop(0, planes // group, early_group, 0)
    take(count + len(phases[2]))
    joined(phases[2])
    take(2 * zs)

    halves(2 * zs)

    def pull_group(step, _):
        g = jnp.where(step < 2, step + 2, 3 - step) if xs == 4 else step
        half = pl.ds(g * (group // 2), group // 2)
        pulled = pull(g, split, 3 * sources)
        out_send[half] = out_send[half] + pulled if early else pulled
        for u in (2, 1, 3, 0):
            t = g * group + u
            i, j = t // Y, lax.rem(t, Y)

            @pl.when(t != 0)
            def _():
                remote(
                    out_send.at[t // 2, :, lax.rem(t, 2)], out_recv.at[plane_back(i, j) - 1],
                    rs_send, rs_recv, plane_peer(i, j)[0],
                ).start()

        return 0

    lax.fori_loop(0, planes // group, pull_group, 0)

    lanes8 = lane_iota((8, 128))
    for t in plane + [0]:
        tile = jnp.zeros((8, 128), jnp.float32)
        for u in range(n // 8):
            for k in range(9):
                total_k = jnp.sum(lane_sums[k, t * n + 8 * u:t * n + 8 * u + 8, :], axis=1, keepdims=True)
                tile = jnp.where(lanes8 == 16 * u + k, total_k, tile)
        ext_send[t] = tile
        if t:
            remote(
                ext_send.at[t], ext_recv.at[plane_back(t // Y, t % Y) - 1], ex_send, ex_recv,
                plane_peer(t // Y, t % Y)[0],
            ).start()
    ext_all = remote(ext_recv, ext_recv, ex_send, ex_recv, sibling)
    pending.append(ext_all.wait_send)

    out_all = remote(out_recv, out_recv, rs_send, rs_recv, sibling)
    pending.append(out_all.wait_send)
    ext_all.wait_recv()
    extra = ext_send[0]
    for t in range(planes - 1):
        extra = extra + ext_recv[t]
    extra = jnp.concatenate(
        [pltpu.roll(extra, 128 - 16 * u, 1) if u else extra for u in range(n // 8)], axis=0
    )
    acceleration = extra.T[0:3, :]
    new_velocities = vel_ref[...] + STEP * acceleration
    nvel_ref[...] = new_velocities
    npos_ref[...] = pos_half + HALF * new_velocities
    index = {}
    for a in range(3):
        for e in range(a, 3):
            index[a, e] = index[e, a] = 3 + len(set(index.values()))
    offset = []
    for a in range(3):
        taken = 0.0
        for e in range(3):
            taken = taken + extra[:, index[a, e]:index[a, e] + 1] * dx_buf[0, 0, e * n:(e + 1) * n, :]
        offset.append(taken)

    out_all.wait_recv()
    for a in range(3):
        pulled = out_send[0, a, 0]
        for t in range(planes - 1):
            pulled = pulled + out_recv[t, a]
        dv_new = tan_ref[3 + a] + STEP * (pulled - offset[a])
        mat_ref[3 + a] = dv_new
        mat_ref[a] = dx_buf[0, 0, a * n:(a + 1) * n, :] + HALF * dv_new
    matrix = mat_ref[...].reshape(6 * n, 128)
    gram = lax.dot_general(
        matrix, matrix, (((0,), (0,)), ((), ())), precision=HIGHEST, preferred_element_type=jnp.float32
    )

    part_rows = 64 // planes
    g_own[...] = gram.reshape(2 * planes, part_rows, 128)
    for t, other in both:
        device, place, there = plane_peer(t // Y, t % Y, other)
        remote(
            g_own.at[there * planes + place], g_plane.at[plane_back(t // Y, t % Y) * 2 + other - 1],
            gs_send.at[0], gs_recv.at[0], device,
        ).start()
    plane_sums = remote(g_plane, g_plane, gs_send.at[0], gs_recv.at[0], sibling)
    pending.append(plane_sums.wait_send)
    plane_sums.wait_recv()
    own = core * planes + here
    mine = g_own[own]
    for t in range(2 * planes - 1):
        mine = mine + g_plane[t]
    g_mine[...] = mine
    for r in line:
        remote(g_mine, g_line.at[zs - r - 1], gs_send.at[1], gs_recv.at[1], line_peer(r)).start()
    line_sums = remote(g_line, g_line, gs_send.at[1], gs_recv.at[1], sibling)
    pending.append(line_sums.wait_send)
    line_sums.wait_recv()
    for r in range(zs - 1):
        mine = mine + g_line[r]
    g_all[own] = mine / (6.0 * total)
    for t, other in both:
        remote(
            g_all.at[own], g_all.at[own], gs_send.at[2], gs_recv.at[2], plane_peer(t // Y, t % Y, other)[0]
        ).start()
    whole = g_all.at[pl.ds(0, 2 * planes - 1)]
    whole = remote(whole, whole, gs_send.at[2], gs_recv.at[2], sibling)
    pending.append(whole.wait_send)
    whole.wait_recv()
    gram_ref[...] = g_all[...].reshape(128, 128)

    for wait in pending:
        wait()


def factor_kernel(gram_ref, mat_ref, npos_ref, nvel_ref, pos_out, vel_out, basis_out, growth_out):
    k = gram_ref.shape[0]
    count = k // 8
    pos_out[...] = npos_ref[...]
    vel_out[...] = nvel_ref[...]
    lanes = lane_iota((8, k))
    rows = lax.broadcasted_iota(jnp.int32, (8, k), 0)
    a = [gram_ref[8 * i:8 * i + 8, :] for i in range(count)]
    q = [jnp.where(lanes == rows + 8 * i, 1.0, 0.0) for i in range(count)]
    full = lambda row: jnp.broadcast_to(row, (8, k))
    inverse_rows = []
    for b in range(count):
        c = {
            i: [jnp.broadcast_to(a[i][:, 8 * b + e:8 * b + e + 1], (8, k)) for e in range(8)]
            for i in range(b, count)
        }
        scale = jnp.ones((8, k), jnp.float32)
        for r in range(8):
            arow, qrow = full(a[b][r:r + 1, :]), full(q[b][r:r + 1, :])
            crow = {e: full(c[b][e][r:r + 1, :]) for e in range(r, 8)}
            scale = jnp.where(rows == r, lax.rsqrt(crow[r]), scale)
            inverse = 1.0 / crow[r]
            for i in range(b, count):
                m = c[i][r] * inverse
                if i == b:
                    m = jnp.where(rows > r, m, 0.0)
                a[i] = a[i] - m * arow
                q[i] = q[i] - m * qrow
                for e in range(r + 1, 8):
                    c[i][e] = c[i][e] - m * crow[e]
        growth_out[8 * b:8 * b + 8, :] = jnp.where(lanes >= rows + 8 * b, a[b] * scale, 0.0)
        inverse_rows.append(q[b] * scale)
    inverse = jnp.concatenate(inverse_rows, axis=0)
    matrix = mat_ref[...].reshape(-1, k)
    basis = lax.dot_general(
        matrix, inverse, (((1,), (1,)), ((), ())), precision=HIGHEST, preferred_element_type=jnp.float32
    )
    basis_out[...] = basis.reshape(basis_out.shape)


def body(positions, velocities, masses, tangents):
    n, k = positions.shape[1], tangents.shape[2]
    xs, zs = lax.axis_size("blk") // 4, lax.axis_size("lane") // 2
    planes = xs * Y
    total = float(n * planes * zs * 2)
    targets, sources = planes * n, 2 * zs * n
    f32, bf16 = jnp.float32, jnp.bfloat16
    vmem = pl.BlockSpec(memory_space=pltpu.VMEM)
    dma = pltpu.SemaphoreType.DMA
    part_rows = 64 // planes
    scratch = [
        pltpu.VMEM((3, n), f32),
        pltpu.VMEM((3, n), f32),
        pltpu.VMEM((1, n), f32),
        pltpu.VMEM((6, n, k), f32),
        dma((4,)),
        pltpu.VMEM((planes, 4, 128), f32),
        pltpu.VMEM((2, zs, 3 * n + 8, k), f32),
        pltpu.VMEM((4, sources), f32),
        pltpu.VMEM((3, targets, 128), f32),
        pltpu.VMEM((3 * targets, 3 * sources), bf16),
        pltpu.VMEM((3 * targets, 3 * sources), bf16),
        pltpu.VMEM((3 * sources, 2 * k), bf16),
        pltpu.VMEM((9, targets, 128), f32),
        pltpu.VMEM((planes, 8, 128), f32),
        pltpu.VMEM((planes - 1, 8, 128), f32),
        pltpu.VMEM((planes // 2, 3, 2, n, k), f32),
        pltpu.VMEM((planes - 1, 3, n, k), f32),
        pltpu.VMEM((2 * planes, part_rows, k), f32),
        pltpu.VMEM((2 * planes - 1, part_rows, k), f32),
        pltpu.VMEM((part_rows, k), f32),
        pltpu.VMEM((zs - 1, part_rows, k), f32),
        pltpu.VMEM((2 * planes, part_rows, k), f32),
        dma, dma,
        dma((zs,)), dma((zs,)),
        dma((zs,)), dma((zs,)),
        dma, dma, dma, dma, dma((3,)), dma((3,)),
    ]
    gram, matrix, npos, nvel = pl.pallas_call(
        functools.partial(step_kernel, xs, zs, n, total),
        out_shape=[
            jax.ShapeDtypeStruct((k, k), f32),
            jax.ShapeDtypeStruct((6, n, k), f32),
            jax.ShapeDtypeStruct((3, n), f32),
            jax.ShapeDtypeStruct((3, n), f32),
        ],
        in_specs=[pl.BlockSpec(memory_space=pltpu.HBM)] * 4,
        out_specs=[vmem] * 4,
        scratch_shapes=scratch,
        compiler_params=pltpu.CompilerParams(
            collective_id=0, has_side_effects=True, vmem_limit_bytes=40 * 1024 * 1024
        ),
    )(*[
        pltpu.with_memory_space_constraint(array, pltpu.HBM)
        for array in (positions, velocities, masses.reshape(1, n), tangents)
    ])
    npos, nvel, basis, growth = pl.pallas_call(
        factor_kernel,
        out_shape=[
            jax.ShapeDtypeStruct((3, n), f32),
            jax.ShapeDtypeStruct((3, n), f32),
            jax.ShapeDtypeStruct((6, n, k), f32),
            jax.ShapeDtypeStruct((k, k), f32),
        ],
        in_specs=[vmem] * 4,
        out_specs=[vmem] * 4,
        compiler_params=pltpu.CompilerParams(vmem_limit_bytes=40 * 1024 * 1024),
    )(gram, matrix, npos, nvel)
    return (npos, nvel, basis, growth)


def solution(mesh):
    return jax.shard_map(
        body,
        mesh=mesh,
        in_specs=(
            P(None, ("blk", "lane")),
            P(None, ("blk", "lane")),
            P(("blk", "lane")),
            P(None, ("blk", "lane"), None),
        ),
        out_specs=(
            P(None, ("blk", "lane")),
            P(None, ("blk", "lane")),
            P(None, ("blk", "lane"), None),
            P(),
        ),
        check_vma=False,
    )
```

```python
import functools

import jax
import jax.numpy as jnp
from jax import lax
from jax.experimental import pallas as pl
from jax.experimental.pallas import tpu as pltpu
from jax.sharding import PartitionSpec as P

STEP = 0.0625
SOFT = 0.0025
HALF = 0.5 * STEP
MESH = pl.DeviceIdType.MESH
HIGHEST = lax.Precision.HIGHEST
Y = 4


RING = {
    16: (
        {0: (3, -3, 1, -1), 3: (6, 2, 4), -3: (-6, -2, -4), 6: (8, 5, 7), -6: (-5, -7)},
        ((0, 3, -3, 1, -1), (2, -2, 4, -4), (6, -6), (5, -5, 7, -7, 8)),
        3,
    ),
    4: ({0: (1, -1), 1: (2,)}, ((0,), (1,), (-1,), (2,)), 1),
}


def lane_iota(shape):
    return lax.broadcasted_iota(jnp.int32, shape, 1)


def pack_lanes(tile_of, count, width, chunk):
    lanes = lane_iota((4, 128))
    total = jnp.zeros((4, 128), jnp.float32)
    for index in range(128 * chunk // width, min(count, (128 * chunk + 127) // width + 1)):
        first, offset = divmod(index * width, 128)
        turned = pltpu.roll(tile_of(index), offset, 1) if offset else tile_of(index)
        if offset + width > 128:
            turned = jnp.where((lanes >= offset) if first == chunk else (lanes < offset), turned, 0.0)
        total = total + turned
    return total


def step_kernel(
    xs, zs, n, total,
    pos_hbm, vel_hbm, mass_hbm, tan_hbm,
    gram_ref, mat_ref, npos_ref, nvel_ref,
    pos_ref, vel_ref, mass_ref, tan_ref, in_sem,
    row_p, dx_buf, src, tgt, k_hi, k_lo, dx_b,
    lane_sums, ext_send, ext_recv, out_send, out_recv,
    g_own, g_plane, g_mine, g_line, g_all,
    pp_send, pp_recv,
    hop_send, hop_recv, sh_send, sh_recv,
    ex_send, ex_recv, rs_send, rs_recv, gs_send, gs_recv,
):
    blk, lane = lax.axis_index("blk"), lax.axis_index("lane")
    core = lax.rem(blk, 2)
    px = blk // 4
    py = lax.rem(lane, 2) * 2 + lax.rem(blk // 2, 2)
    z = lane // 2
    planes = xs * Y
    targets = planes * n
    sources = 2 * zs * n
    passes, phases, reach = RING[zs]
    order = [(h, place) for group in phases for h in range(2) for place in group]
    early = 2 * (zs - len(phases[3])) * n // 128
    split = 3 * 128 * early
    width = sources // 128 - early

    def column(b, chunk):
        return 128 * (b * early + chunk) if chunk < early else split + 128 * (b * width + chunk - early)

    def plane_peer(i, j, other=0):
        ox, oy = lax.rem(px + i, xs), lax.rem(py + j, Y)
        there = 1 - core if other else core
        return (ox * 4 + lax.rem(oy, 2) * 2 + there, z * 2 + oy // 2), ox * Y + oy, there

    def plane_back(i, j):
        return lax.rem(xs - i, xs) * Y + lax.rem(Y - j, Y)

    def away(length, r):
        return min(r, length - r)

    line = sorted(range(1, zs), key=lambda r: -away(zs, r))
    plane = sorted(range(1, planes), key=lambda t: -away(xs, t // Y) - away(Y, t % Y))
    both = [(t, other) for t in plane for other in range(2)] + [(0, 1)]

    def line_peer(r):
        return (blk, lax.rem(z + r, zs) * 2 + lax.rem(lane, 2))

    sibling = (blk + 1 - 2 * core, lane)
    here = px * Y + py

    def remote(source, target, send_sem, recv_sem, device):
        return pltpu.make_async_remote_copy(
            src_ref=source, dst_ref=target, send_sem=send_sem, recv_sem=recv_sem,
            device_id=device, device_id_type=MESH,
        )

    loads = [
        pltpu.make_async_copy(source, target, in_sem.at[index])
        for index, (source, target) in enumerate(
            [(pos_hbm, pos_ref), (vel_hbm, vel_ref), (mass_hbm, mass_ref), (tan_hbm, tan_ref)]
        )
    ]
    for load in loads:
        load.start()
    barrier = pltpu.get_barrier_semaphore()
    near = sorted({r % zs for r in range(-reach, reach + 1)} - {0}, key=lambda r: -away(zs, r))
    for r in near:
        pl.semaphore_signal(barrier, inc=1, device_id=line_peer(r), device_id_type=MESH)
    for t in plane:
        pl.semaphore_signal(barrier, inc=1, device_id=plane_peer(t // Y, t % Y)[0], device_id_type=MESH)
    pl.semaphore_signal(barrier, inc=1, device_id=sibling, device_id_type=MESH)

    for load in loads:
        load.wait()
    pos_half = pos_ref[...] + HALF * vel_ref[...]
    row_p[0] = jnp.zeros((4, 128), jnp.float32)
    row_p[0, 0:3, 0:n] = pos_half
    row_p[0, 3:4, 0:n] = mass_ref[...] / total
    dx_half = tan_ref[0:3] + HALF * tan_ref[3:6]
    dx_buf[0, 0, 0:3 * n] = dx_half.reshape(3 * n, 128)
    dx_buf[0, 0, 3 * n:3 * n + 4] = row_p[0]
    dx_buf[0, 0, 3 * n + 4:3 * n + 8] = jnp.zeros((4, 128), jnp.float32)
    pl.semaphore_wait(barrier, len(near) + planes)

    pending = []
    plane_slots = row_p.at[pl.ds(1, planes - 1)]
    plane_all = remote(plane_slots, plane_slots, pp_send, pp_recv, sibling)

    def begin(copy):
        copy.start()
        pending.append(copy.wait_send)

    def hop(start, end):
        return remote(
            dx_buf.at[0, -start % zs], dx_buf.at[0, -end % zs],
            hop_send.at[end % zs], hop_recv.at[end % zs], line_peer((end - start) % zs),
        )

    before = {end: start for start, ends in passes.items() for end in ends}

    def share(r):
        return remote(dx_buf.at[0, r], dx_buf.at[1, r], sh_send.at[r], sh_recv.at[r], sibling)

    def visit(place):
        if place:
            hop(before[place], place).wait_recv()
        for end in passes.get(place, ()):
            begin(hop(place, end))
        begin(share(-place % zs))

    def joined(group):
        for place in group:
            share(-place % zs).wait_recv()

    def pack_sources(chunks):
        def tile_of(q):
            h, place = order[q]
            return dx_buf[h, -place % zs, 3 * n:3 * n + 4, :]

        for chunk in chunks:
            src[:, 128 * chunk:128 * chunk + 128] = pack_lanes(tile_of, 2 * zs, n, chunk)

    visit(0)
    for t in plane:
        remote(row_p.at[0], row_p.at[plane_back(t // Y, t % Y)], pp_send, pp_recv, plane_peer(t // Y, t % Y)[0]).start()
    pending.append(plane_all.wait_send)
    for place in phases[0][1:]:
        visit(place)
    plane_all.wait_recv()
    for c in range((targets + 127) // 128):
        piece = pack_lanes(lambda t: row_p[t], planes, n, c)
        columns = jnp.concatenate([piece, piece], axis=0).T
        last = min(128, targets - c * 128)
        for a in range(3):
            tgt[a, c * 128:c * 128 + last, :] = jnp.broadcast_to(columns[0:last, a:a + 1], (last, 128))
    def pair_block(chunks, pair, _):
        where = pl.ds(pl.multiple_of(pair * 2 * n, 16), 2 * n)
        base = pair * (6 * n)
        own = [tgt[a, where, :] for a in range(3)]
        sums = [None if chunks[0] == 0 else lane_sums[k, where, :] for k in range(9)]
        for c in chunks:
            columns = pl.ds(c * 128, 128)
            d = [src[a:a + 1, columns] - own[a] for a in range(3)]
            squared = d[0] * d[0] + d[1] * d[1] + d[2] * d[2] + SOFT
            inverse = lax.rsqrt(squared)
            inverse2 = inverse * inverse
            near = src[3:4, columns] * inverse * inverse2
            tide = 3.0 * near * inverse2
            td = [tide * d[a] for a in range(3)]
            part = {}
            for a in range(3):
                for e in range(a, 3):
                    product = td[a] * d[e]
                    part[a, e] = near - product if a == e else -product
            terms = [near * d[a] for a in range(3)] + [part[a, e] for a in range(3) for e in range(a, 3)]
            sums = [t if s is None else s + t for s, t in zip(sums, terms)]
            for a in range(3):
                for e in range(a, 3):
                    high = part[a, e].astype(jnp.bfloat16)
                    low = (part[a, e] - high.astype(jnp.float32)).astype(jnp.bfloat16)
                    for f, g in {(a, e), (e, a)}:
                        to = (pl.ds(pl.multiple_of(base + f * 2 * n, 16), 2 * n), pl.ds(column(g, c), 128))
                        k_hi[to] = high
                        k_lo[to] = low
        for k in range(9):
            lane_sums[k, where, :] = sums[k]
        return 0

    progress = [0, 0]

    def take(count):
        chunks = range(progress[0], count * n // 128)
        if len(chunks):
            progress[0] = chunks[-1] + 1
            pack_sources(chunks)
            lax.fori_loop(0, planes // 2, functools.partial(pair_block, list(chunks)), 0, unroll=2)

    def halves(count):
        for q in range(progress[1], count, 2):
            for b in range(3):
                block = jnp.concatenate(
                    [dx_buf[h, -place % zs, b * n:(b + 1) * n, :] for h, place in order[q:q + 2]], axis=0
                )
                first = q * n
                while first < (q + 2) * n:
                    last = min((q + 2) * n, first // 128 * 128 + 128)
                    part = block[first - q * n:last - q * n, :]
                    high = part.astype(jnp.bfloat16)
                    low = (part - high.astype(jnp.float32)).astype(jnp.bfloat16)
                    start = column(b, first // 128) + first % 128
                    dx_b[start:start + last - first, 0:128] = high
                    dx_b[start:start + last - first, 128:256] = low
                    first = last
        progress[1] = count

    group = 4
    rows = group * 3 * n

    def pull(g, low, high):
        where = pl.ds(pl.multiple_of(g * rows, 16), rows)
        first = jnp.dot(k_hi[where, low:high], dx_b[low:high, :], preferred_element_type=jnp.float32)
        second = jnp.dot(k_lo[where, low:high], dx_b[low:high, 0:128], preferred_element_type=jnp.float32)
        pulled = first[:, 0:128] + (first[:, 128:256] + second)
        return pulled.reshape(group // 2, 3, 2, n, 128)

    def early_group(g, _):
        out_send[pl.ds(g * (group // 2), group // 2)] = pull(g, 0, split)
        return 0

    joined(phases[0])
    count = 2 * len(phases[0])
    take(count)
    for place in phases[1] + phases[2]:
        visit(place)
    for group_of in phases[1:3]:
        joined(group_of)
        count += 2 * len(group_of)
        take(count)
    halves(count)
    if early:
        lax.fori_loop(0, planes // group, early_group, 0)
    for place in phases[3]:
        visit(place)
    take(count + len(phases[3]))
    joined(phases[3])
    take(2 * zs)

    halves(2 * zs)

    def pull_group(step, _):
        g = jnp.where(step < 2, step + 2, 3 - step) if xs == 4 else step
        half = pl.ds(g * (group // 2), group // 2)
        pulled = pull(g, split, 3 * sources)
        out_send[half] = out_send[half] + pulled if early else pulled
        for u in (2, 1, 3, 0):
            t = g * group + u
            i, j = t // Y, lax.rem(t, Y)

            @pl.when(t != 0)
            def _():
                remote(
                    out_send.at[t // 2, :, lax.rem(t, 2)], out_recv.at[plane_back(i, j) - 1],
                    rs_send, rs_recv, plane_peer(i, j)[0],
                ).start()

        return 0

    lax.fori_loop(0, planes // group, pull_group, 0)

    lanes8 = lane_iota((8, 128))
    for t in plane + [0]:
        tile = jnp.zeros((8, 128), jnp.float32)
        for u in range(n // 8):
            for k in range(9):
                total_k = jnp.sum(lane_sums[k, t * n + 8 * u:t * n + 8 * u + 8, :], axis=1, keepdims=True)
                tile = jnp.where(lanes8 == 16 * u + k, total_k, tile)
        ext_send[t] = tile
        if t:
            remote(
                ext_send.at[t], ext_recv.at[plane_back(t // Y, t % Y) - 1], ex_send, ex_recv,
                plane_peer(t // Y, t % Y)[0],
            ).start()
    ext_all = remote(ext_recv, ext_recv, ex_send, ex_recv, sibling)
    pending.append(ext_all.wait_send)

    out_all = remote(out_recv, out_recv, rs_send, rs_recv, sibling)
    pending.append(out_all.wait_send)
    ext_all.wait_recv()
    extra = ext_send[0]
    for t in range(planes - 1):
        extra = extra + ext_recv[t]
    extra = jnp.concatenate(
        [pltpu.roll(extra, 128 - 16 * u, 1) if u else extra for u in range(n // 8)], axis=0
    )
    acceleration = extra.T[0:3, :]
    new_velocities = vel_ref[...] + STEP * acceleration
    nvel_ref[...] = new_velocities
    npos_ref[...] = pos_half + HALF * new_velocities
    index = {}
    for a in range(3):
        for e in range(a, 3):
            index[a, e] = index[e, a] = 3 + len(set(index.values()))
    offset = []
    for a in range(3):
        taken = 0.0
        for e in range(3):
            taken = taken + extra[:, index[a, e]:index[a, e] + 1] * dx_buf[0, 0, e * n:(e + 1) * n, :]
        offset.append(taken)

    out_all.wait_recv()
    for a in range(3):
        pulled = out_send[0, a, 0]
        for t in range(planes - 1):
            pulled = pulled + out_recv[t, a]
        dv_new = tan_ref[3 + a] + STEP * (pulled - offset[a])
        mat_ref[3 + a] = dv_new
        mat_ref[a] = dx_buf[0, 0, a * n:(a + 1) * n, :] + HALF * dv_new
    matrix = mat_ref[...].reshape(6 * n, 128)
    gram = lax.dot_general(
        matrix, matrix, (((0,), (0,)), ((), ())), precision=HIGHEST, preferred_element_type=jnp.float32
    )

    part_rows = 64 // planes
    g_own[...] = gram.reshape(2 * planes, part_rows, 128)
    for t, other in both:
        device, place, there = plane_peer(t // Y, t % Y, other)
        remote(
            g_own.at[there * planes + place], g_plane.at[plane_back(t // Y, t % Y) * 2 + other - 1],
            gs_send.at[0], gs_recv.at[0], device,
        ).start()
    plane_sums = remote(g_plane, g_plane, gs_send.at[0], gs_recv.at[0], sibling)
    pending.append(plane_sums.wait_send)
    plane_sums.wait_recv()
    own = core * planes + here
    mine = g_own[own]
    for t in range(2 * planes - 1):
        mine = mine + g_plane[t]
    g_mine[...] = mine
    for r in line:
        remote(g_mine, g_line.at[zs - r - 1], gs_send.at[1], gs_recv.at[1], line_peer(r)).start()
    line_sums = remote(g_line, g_line, gs_send.at[1], gs_recv.at[1], sibling)
    for wait in pending:
        wait()
    pending = [line_sums.wait_send]
    line_sums.wait_recv()
    for r in range(zs - 1):
        mine = mine + g_line[r]
    g_all[own] = mine / (6.0 * total)
    for t, other in both:
        remote(
            g_all.at[own], g_all.at[own], gs_send.at[2], gs_recv.at[2], plane_peer(t // Y, t % Y, other)[0]
        ).start()
    whole = g_all.at[pl.ds(0, 2 * planes - 1)]
    whole = remote(whole, whole, gs_send.at[2], gs_recv.at[2], sibling)
    pending.append(whole.wait_send)
    whole.wait_recv()
    gram_ref[...] = g_all[...].reshape(128, 128)

    for wait in pending:
        wait()


def factor_kernel(gram_ref, mat_ref, npos_ref, nvel_ref, pos_out, vel_out, basis_out, growth_out):
    k = gram_ref.shape[0]
    count = k // 8
    pos_out[...] = npos_ref[...]
    vel_out[...] = nvel_ref[...]
    lanes = lane_iota((8, k))
    rows = lax.broadcasted_iota(jnp.int32, (8, k), 0)
    a = [gram_ref[8 * i:8 * i + 8, :] for i in range(count)]
    q = [jnp.where(lanes == rows + 8 * i, 1.0, 0.0) for i in range(count)]
    full = lambda row: jnp.broadcast_to(row, (8, k))
    inverse_rows = []
    for b in range(count):
        c = {
            i: [jnp.broadcast_to(a[i][:, 8 * b + e:8 * b + e + 1], (8, k)) for e in range(8)]
            for i in range(b, count)
        }
        scale = jnp.ones((8, k), jnp.float32)
        for r in range(8):
            arow, qrow = full(a[b][r:r + 1, :]), full(q[b][r:r + 1, :])
            crow = {e: full(c[b][e][r:r + 1, :]) for e in range(r, 8)}
            root = lax.rsqrt(crow[r])
            scale = jnp.where(rows == r, root, scale)
            inverse = root * root
            for i in range(b, count):
                m = c[i][r] * inverse
                if i == b:
                    m = jnp.where(rows > r, m, 0.0)
                a[i] = a[i] - m * arow
                q[i] = q[i] - m * qrow
                for e in range(r + 1, 8):
                    c[i][e] = c[i][e] - m * crow[e]
        growth_out[8 * b:8 * b + 8, :] = jnp.where(lanes >= rows + 8 * b, a[b] * scale, 0.0)
        inverse_rows.append(q[b] * scale)
    inverse = jnp.concatenate(inverse_rows, axis=0)
    matrix = mat_ref[...].reshape(-1, k)
    basis = lax.dot_general(
        matrix, inverse, (((1,), (1,)), ((), ())), precision=HIGHEST, preferred_element_type=jnp.float32
    )
    basis_out[...] = basis.reshape(basis_out.shape)


def body(positions, velocities, masses, tangents):
    n, k = positions.shape[1], tangents.shape[2]
    xs, zs = lax.axis_size("blk") // 4, lax.axis_size("lane") // 2
    planes = xs * Y
    total = float(n * planes * zs * 2)
    targets, sources = planes * n, 2 * zs * n
    f32, bf16 = jnp.float32, jnp.bfloat16
    vmem = pl.BlockSpec(memory_space=pltpu.VMEM)
    dma = pltpu.SemaphoreType.DMA
    part_rows = 64 // planes
    scratch = [
        pltpu.VMEM((3, n), f32),
        pltpu.VMEM((3, n), f32),
        pltpu.VMEM((1, n), f32),
        pltpu.VMEM((6, n, k), f32),
        dma((4,)),
        pltpu.VMEM((planes, 4, 128), f32),
        pltpu.VMEM((2, zs, 3 * n + 8, k), f32),
        pltpu.VMEM((4, sources), f32),
        pltpu.VMEM((3, targets, 128), f32),
        pltpu.VMEM((3 * targets, 3 * sources), bf16),
        pltpu.VMEM((3 * targets, 3 * sources), bf16),
        pltpu.VMEM((3 * sources, 2 * k), bf16),
        pltpu.VMEM((9, targets, 128), f32),
        pltpu.VMEM((planes, 8, 128), f32),
        pltpu.VMEM((planes - 1, 8, 128), f32),
        pltpu.VMEM((planes // 2, 3, 2, n, k), f32),
        pltpu.VMEM((planes - 1, 3, n, k), f32),
        pltpu.VMEM((2 * planes, part_rows, k), f32),
        pltpu.VMEM((2 * planes - 1, part_rows, k), f32),
        pltpu.VMEM((part_rows, k), f32),
        pltpu.VMEM((zs - 1, part_rows, k), f32),
        pltpu.VMEM((2 * planes, part_rows, k), f32),
        dma, dma,
        dma((zs,)), dma((zs,)),
        dma((zs,)), dma((zs,)),
        dma, dma, dma, dma, dma((3,)), dma((3,)),
    ]
    gram, matrix, npos, nvel = pl.pallas_call(
        functools.partial(step_kernel, xs, zs, n, total),
        out_shape=[
            jax.ShapeDtypeStruct((k, k), f32),
            jax.ShapeDtypeStruct((6, n, k), f32),
            jax.ShapeDtypeStruct((3, n), f32),
            jax.ShapeDtypeStruct((3, n), f32),
        ],
        in_specs=[pl.BlockSpec(memory_space=pltpu.HBM)] * 4,
        out_specs=[vmem] * 4,
        scratch_shapes=scratch,
        compiler_params=pltpu.CompilerParams(
            collective_id=0, has_side_effects=True, vmem_limit_bytes=40 * 1024 * 1024
        ),
    )(*[
        pltpu.with_memory_space_constraint(array, pltpu.HBM)
        for array in (positions, velocities, masses.reshape(1, n), tangents)
    ])
    npos, nvel, basis, growth = pl.pallas_call(
        factor_kernel,
        out_shape=[
            jax.ShapeDtypeStruct((3, n), f32),
            jax.ShapeDtypeStruct((3, n), f32),
            jax.ShapeDtypeStruct((6, n, k), f32),
            jax.ShapeDtypeStruct((k, k), f32),
        ],
        in_specs=[vmem] * 4,
        out_specs=[vmem] * 4,
        compiler_params=pltpu.CompilerParams(vmem_limit_bytes=40 * 1024 * 1024),
    )(gram, matrix, npos, nvel)
    return (npos, nvel, basis, growth)


def solution(mesh):
    return jax.shard_map(
        body,
        mesh=mesh,
        in_specs=(
            P(None, ("blk", "lane")),
            P(None, ("blk", "lane")),
            P(("blk", "lane")),
            P(None, ("blk", "lane"), None),
        ),
        out_specs=(
            P(None, ("blk", "lane")),
            P(None, ("blk", "lane")),
            P(None, ("blk", "lane"), None),
            P(),
        ),
        check_vma=False,
    )
```

```python
import functools

import jax
import jax.numpy as jnp
from jax import lax
from jax.experimental import pallas as pl
from jax.experimental.pallas import tpu as pltpu
from jax.sharding import PartitionSpec as P

STEP = 0.0625
SOFT = 0.0025
HALF = 0.5 * STEP
MESH = pl.DeviceIdType.MESH
HIGHEST = lax.Precision.HIGHEST
Y = 4


RING = {
    16: (
        {0: (3, -3, 1, -1), 3: (6, 2, 4), -3: (-6, -2, -4), 6: (8, 5, 7), -6: (-5, -7)},
        ((0, 3, -3, 1, -1), (2, -2, 4, -4), (6, -6), (5, -5, 7, -7, 8)),
        3,
    ),
    4: ({0: (1, -1), 1: (2,)}, ((0,), (1,), (-1,), (2,)), 1),
}


def lane_iota(shape):
    return lax.broadcasted_iota(jnp.int32, shape, 1)


def pack_lanes(tile_of, count, width, chunk):
    lanes = lane_iota((4, 128))
    total = jnp.zeros((4, 128), jnp.float32)
    for index in range(128 * chunk // width, min(count, (128 * chunk + 127) // width + 1)):
        first, offset = divmod(index * width, 128)
        turned = pltpu.roll(tile_of(index), offset, 1) if offset else tile_of(index)
        if offset + width > 128:
            turned = jnp.where((lanes >= offset) if first == chunk else (lanes < offset), turned, 0.0)
        total = total + turned
    return total


def step_kernel(
    xs, zs, n, total,
    pos_hbm, vel_hbm, mass_hbm, tan_hbm,
    gram_ref, mat_ref, npos_ref, nvel_ref,
    pos_ref, vel_ref, mass_ref, tan_ref, in_sem,
    row_p, dx_buf, src, tgt, k_hi, k_lo, dx_b,
    lane_sums, ext_send, ext_recv, out_send, out_recv,
    g_own, g_plane, g_mine, g_line, g_all,
    pp_send, pp_recv,
    hop_send, hop_recv, sh_send, sh_recv,
    ex_send, ex_recv, rs_send, rs_recv, gs_send, gs_recv,
):
    blk, lane = lax.axis_index("blk"), lax.axis_index("lane")
    core = lax.rem(blk, 2)
    px = blk // 4
    py = lax.rem(lane, 2) * 2 + lax.rem(blk // 2, 2)
    z = lane // 2
    planes = xs * Y
    targets = planes * n
    sources = 2 * zs * n
    passes, phases, reach = RING[zs]
    order = [(h, place) for group in phases for h in range(2) for place in group]
    early = 2 * (zs - len(phases[3])) * n // 128
    split = 3 * 128 * early
    width = sources // 128 - early

    def column(b, chunk):
        return 128 * (b * early + chunk) if chunk < early else split + 128 * (b * width + chunk - early)

    def plane_peer(i, j, other=0):
        ox, oy = lax.rem(px + i, xs), lax.rem(py + j, Y)
        there = 1 - core if other else core
        return (ox * 4 + lax.rem(oy, 2) * 2 + there, z * 2 + oy // 2), ox * Y + oy, there

    def plane_back(i, j):
        return lax.rem(xs - i, xs) * Y + lax.rem(Y - j, Y)

    def away(length, r):
        return min(r, length - r)

    line = sorted(range(1, zs), key=lambda r: -away(zs, r))
    plane = sorted(range(1, planes), key=lambda t: -away(xs, t // Y) - away(Y, t % Y))
    both = [(t, other) for t in plane for other in range(2)] + [(0, 1)]

    def line_peer(r):
        return (blk, lax.rem(z + r, zs) * 2 + lax.rem(lane, 2))

    sibling = (blk + 1 - 2 * core, lane)
    here = px * Y + py

    def remote(source, target, send_sem, recv_sem, device):
        return pltpu.make_async_remote_copy(
            src_ref=source, dst_ref=target, send_sem=send_sem, recv_sem=recv_sem,
            device_id=device, device_id_type=MESH,
        )

    loads = [
        pltpu.make_async_copy(source, target, in_sem.at[index])
        for index, (source, target) in enumerate(
            [(pos_hbm, pos_ref), (vel_hbm, vel_ref), (mass_hbm, mass_ref), (tan_hbm, tan_ref)]
        )
    ]
    for load in loads:
        load.start()
    barrier = pltpu.get_barrier_semaphore()
    near = sorted({r % zs for r in range(-reach, reach + 1)} - {0}, key=lambda r: -away(zs, r))
    for r in near:
        pl.semaphore_signal(barrier, inc=1, device_id=line_peer(r), device_id_type=MESH)
    for t in plane:
        pl.semaphore_signal(barrier, inc=1, device_id=plane_peer(t // Y, t % Y)[0], device_id_type=MESH)
    pl.semaphore_signal(barrier, inc=1, device_id=sibling, device_id_type=MESH)

    for load in loads:
        load.wait()
    pos_half = pos_ref[...] + HALF * vel_ref[...]
    row_p[0] = jnp.zeros((4, 128), jnp.float32)
    row_p[0, 0:3, 0:n] = pos_half
    row_p[0, 3:4, 0:n] = mass_ref[...] / total
    dx_half = tan_ref[0:3] + HALF * tan_ref[3:6]
    dx_buf[0, 0, 0:3 * n] = dx_half.reshape(3 * n, 128)
    dx_buf[0, 0, 3 * n:3 * n + 4] = row_p[0]
    dx_buf[0, 0, 3 * n + 4:3 * n + 8] = jnp.zeros((4, 128), jnp.float32)
    pl.semaphore_wait(barrier, len(near) + planes)

    pending = []
    plane_slots = row_p.at[pl.ds(1, planes - 1)]
    plane_all = remote(plane_slots, plane_slots, pp_send, pp_recv, sibling)

    def begin(copy):
        copy.start()
        pending.append(copy.wait_send)

    def hop(start, end):
        return remote(
            dx_buf.at[0, -start % zs], dx_buf.at[0, -end % zs],
            hop_send.at[end % zs], hop_recv.at[end % zs], line_peer((end - start) % zs),
        )

    before = {end: start for start, ends in passes.items() for end in ends}

    def share(r):
        return remote(dx_buf.at[0, r], dx_buf.at[1, r], sh_send.at[r], sh_recv.at[r], sibling)

    def visit(place):
        if place:
            hop(before[place], place).wait_recv()
        for end in passes.get(place, ()):
            begin(hop(place, end))
        begin(share(-place % zs))

    def joined(group):
        for place in group:
            share(-place % zs).wait_recv()

    def pack_sources(chunks):
        def tile_of(q):
            h, place = order[q]
            return dx_buf[h, -place % zs, 3 * n:3 * n + 4, :]

        for chunk in chunks:
            src[:, 128 * chunk:128 * chunk + 128] = pack_lanes(tile_of, 2 * zs, n, chunk)

    visit(0)
    for t in plane:
        remote(row_p.at[0], row_p.at[plane_back(t // Y, t % Y)], pp_send, pp_recv, plane_peer(t // Y, t % Y)[0]).start()
    pending.append(plane_all.wait_send)
    for place in phases[0][1:]:
        visit(place)
    plane_all.wait_recv()
    for c in range((targets + 127) // 128):
        piece = pack_lanes(lambda t: row_p[t], planes, n, c)
        columns = jnp.concatenate([piece, piece], axis=0).T
        last = min(128, targets - c * 128)
        for a in range(3):
            tgt[a, c * 128:c * 128 + last, :] = jnp.broadcast_to(columns[0:last, a:a + 1], (last, 128))
    def pair_block(chunks, pair, _):
        where = pl.ds(pl.multiple_of(pair * 2 * n, 16), 2 * n)
        base = pair * (6 * n)
        own = [tgt[a, where, :] for a in range(3)]
        sums = [None if chunks[0] == 0 else lane_sums[k, where, :] for k in range(9)]
        for c in chunks:
            columns = pl.ds(c * 128, 128)
            d = [src[a:a + 1, columns] - own[a] for a in range(3)]
            squared = d[0] * d[0] + d[1] * d[1] + d[2] * d[2] + SOFT
            inverse = lax.rsqrt(squared)
            inverse2 = inverse * inverse
            near = src[3:4, columns] * inverse * inverse2
            tide = 3.0 * near * inverse2
            td = [tide * d[a] for a in range(3)]
            part = {}
            for a in range(3):
                for e in range(a, 3):
                    product = td[a] * d[e]
                    part[a, e] = near - product if a == e else -product
            terms = [near * d[a] for a in range(3)] + [part[a, e] for a in range(3) for e in range(a, 3)]
            sums = [t if s is None else s + t for s, t in zip(sums, terms)]
            for a in range(3):
                for e in range(a, 3):
                    high = part[a, e].astype(jnp.bfloat16)
                    low = (part[a, e] - high.astype(jnp.float32)).astype(jnp.bfloat16)
                    for f, g in {(a, e), (e, a)}:
                        to = (pl.ds(pl.multiple_of(base + f * 2 * n, 16), 2 * n), pl.ds(column(g, c), 128))
                        k_hi[to] = high
                        k_lo[to] = low
        for k in range(9):
            lane_sums[k, where, :] = sums[k]
        return 0

    progress = [0, 0]

    def take(count):
        chunks = range(progress[0], count * n // 128)
        if len(chunks):
            progress[0] = chunks[-1] + 1
            pack_sources(chunks)
            lax.fori_loop(0, planes // 2, functools.partial(pair_block, list(chunks)), 0, unroll=2)

    def halves(count):
        for q in range(progress[1], count, 2):
            for b in range(3):
                block = jnp.concatenate(
                    [dx_buf[h, -place % zs, b * n:(b + 1) * n, :] for h, place in order[q:q + 2]], axis=0
                )
                first = q * n
                while first < (q + 2) * n:
                    last = min((q + 2) * n, first // 128 * 128 + 128)
                    part = block[first - q * n:last - q * n, :]
                    high = part.astype(jnp.bfloat16)
                    low = (part - high.astype(jnp.float32)).astype(jnp.bfloat16)
                    start = column(b, first // 128) + first % 128
                    dx_b[start:start + last - first, 0:128] = high
                    dx_b[start:start + last - first, 128:256] = low
                    first = last
        progress[1] = count

    group = 4
    rows = group * 3 * n

    def pull(g, low, high):
        where = pl.ds(pl.multiple_of(g * rows, 16), rows)
        first = jnp.dot(k_hi[where, low:high], dx_b[low:high, :], preferred_element_type=jnp.float32)
        second = jnp.dot(k_lo[where, low:high], dx_b[low:high, 0:128], preferred_element_type=jnp.float32)
        pulled = first[:, 0:128] + (first[:, 128:256] + second)
        return pulled.reshape(group // 2, 3, 2, n, 128)

    def early_group(g, _):
        out_send[pl.ds(g * (group // 2), group // 2)] = pull(g, 0, split)
        return 0

    joined(phases[0])
    count = 2 * len(phases[0])
    take(count)
    for place in phases[1] + phases[2]:
        visit(place)
    for group_of in phases[1:3]:
        joined(group_of)
        count += 2 * len(group_of)
        take(count)
    halves(count)
    if early:
        lax.fori_loop(0, planes // group, early_group, 0)
    for place in phases[3]:
        visit(place)
    take(count + len(phases[3]))
    joined(phases[3])
    take(2 * zs)

    halves(2 * zs)

    def pull_group(step, _):
        g = jnp.where(step < 2, step + 2, 3 - step) if xs == 4 else step
        half = pl.ds(g * (group // 2), group // 2)
        pulled = pull(g, split, 3 * sources)
        out_send[half] = out_send[half] + pulled if early else pulled
        for u in (2, 1, 3, 0):
            t = g * group + u
            i, j = t // Y, lax.rem(t, Y)

            @pl.when(t != 0)
            def _():
                remote(
                    out_send.at[t // 2, :, lax.rem(t, 2)], out_recv.at[plane_back(i, j) - 1],
                    rs_send, rs_recv, plane_peer(i, j)[0],
                ).start()

        return 0

    lax.fori_loop(0, planes // group, pull_group, 0)

    lanes8 = lane_iota((8, 128))
    for t in plane + [0]:
        tile = jnp.zeros((8, 128), jnp.float32)
        for u in range(n // 8):
            for k in range(9):
                total_k = jnp.sum(lane_sums[k, t * n + 8 * u:t * n + 8 * u + 8, :], axis=1, keepdims=True)
                tile = jnp.where(lanes8 == 16 * u + k, total_k, tile)
        ext_send[t] = tile
        if t:
            remote(
                ext_send.at[t], ext_recv.at[plane_back(t // Y, t % Y) - 1], ex_send, ex_recv,
                plane_peer(t // Y, t % Y)[0],
            ).start()
    ext_all = remote(ext_recv, ext_recv, ex_send, ex_recv, sibling)
    pending.append(ext_all.wait_send)

    out_all = remote(out_recv, out_recv, rs_send, rs_recv, sibling)
    pending.append(out_all.wait_send)
    ext_all.wait_recv()
    extra = ext_send[0]
    for t in range(planes - 1):
        extra = extra + ext_recv[t]
    extra = jnp.concatenate(
        [pltpu.roll(extra, 128 - 16 * u, 1) if u else extra for u in range(n // 8)], axis=0
    )
    acceleration = extra.T[0:3, :]
    new_velocities = vel_ref[...] + STEP * acceleration
    nvel_ref[...] = new_velocities
    npos_ref[...] = pos_half + HALF * new_velocities
    index = {}
    for a in range(3):
        for e in range(a, 3):
            index[a, e] = index[e, a] = 3 + len(set(index.values()))
    offset = []
    for a in range(3):
        taken = 0.0
        for e in range(3):
            taken = taken + extra[:, index[a, e]:index[a, e] + 1] * dx_buf[0, 0, e * n:(e + 1) * n, :]
        offset.append(taken)

    out_all.wait_recv()
    for a in range(3):
        pulled = out_send[0, a, 0]
        for t in range(planes - 1):
            pulled = pulled + out_recv[t, a]
        dv_new = tan_ref[3 + a] + STEP * (pulled - offset[a])
        mat_ref[3 + a] = dv_new
        mat_ref[a] = dx_buf[0, 0, a * n:(a + 1) * n, :] + HALF * dv_new
    matrix = mat_ref[...].reshape(6 * n, 128)
    gram = lax.dot_general(
        matrix, matrix, (((0,), (0,)), ((), ())), precision=HIGHEST, preferred_element_type=jnp.float32
    )

    part_rows = 64 // planes
    g_own[...] = gram.reshape(2 * planes, part_rows, 128)
    for t, other in both:
        device, place, there = plane_peer(t // Y, t % Y, other)
        remote(
            g_own.at[there * planes + place], g_plane.at[plane_back(t // Y, t % Y) * 2 + other - 1],
            gs_send.at[0], gs_recv.at[0], device,
        ).start()
    plane_sums = remote(g_plane, g_plane, gs_send.at[0], gs_recv.at[0], sibling)
    pending.append(plane_sums.wait_send)
    plane_sums.wait_recv()
    own = core * planes + here
    mine = g_own[own]
    for t in range(2 * planes - 1):
        mine = mine + g_plane[t]
    g_mine[...] = mine
    for r in line:
        remote(g_mine, g_line.at[zs - r - 1], gs_send.at[1], gs_recv.at[1], line_peer(r)).start()
    line_sums = remote(g_line, g_line, gs_send.at[1], gs_recv.at[1], sibling)
    for wait in pending:
        wait()
    pending = [line_sums.wait_send]
    line_sums.wait_recv()
    for r in range(zs - 1):
        mine = mine + g_line[r]
    g_all[own] = mine / (6.0 * total)
    for t, other in both:
        remote(
            g_all.at[own], g_all.at[own], gs_send.at[2], gs_recv.at[2], plane_peer(t // Y, t % Y, other)[0]
        ).start()
    whole = g_all.at[pl.ds(0, 2 * planes - 1)]
    whole = remote(whole, whole, gs_send.at[2], gs_recv.at[2], sibling)
    pending.append(whole.wait_send)
    whole.wait_recv()
    gram_ref[...] = g_all[...].reshape(128, 128)

    for wait in pending:
        wait()


def factor_kernel(gram_ref, mat_ref, npos_ref, nvel_ref, pos_out, vel_out, basis_out, growth_out):
    k = gram_ref.shape[0]
    count = k // 8
    pos_out[...] = npos_ref[...]
    vel_out[...] = nvel_ref[...]
    lanes = lane_iota((8, k))
    rows = lax.broadcasted_iota(jnp.int32, (8, k), 0)
    a = [gram_ref[8 * i:8 * i + 8, :] for i in range(count)]
    q = [jnp.where(lanes == rows + 8 * i, 1.0, 0.0) for i in range(count)]
    full = lambda row: jnp.broadcast_to(row, (8, k))
    inverse_rows = []
    for b in range(count):
        c = {
            i: [jnp.broadcast_to(a[i][:, 8 * b + e:8 * b + e + 1], (8, k)) for e in range(8)]
            for i in range(b, count)
        }
        scale = jnp.ones((8, k), jnp.float32)
        for r in range(8):
            arow, qrow = full(a[b][r:r + 1, :]), full(q[b][r:r + 1, :])
            crow = {e: full(c[b][e][r:r + 1, :]) for e in range(r, 8)}
            scale = jnp.where(rows == r, lax.rsqrt(crow[r]), scale)
            inverse = 1.0 / crow[r]
            for i in range(b, count):
                m = c[i][r] * inverse
                if i == b:
                    m = jnp.where(rows > r, m, 0.0)
                a[i] = a[i] - m * arow
                q[i] = q[i] - m * qrow
                for e in range(r + 1, 8):
                    c[i][e] = c[i][e] - m * crow[e]
        growth_out[8 * b:8 * b + 8, :] = jnp.where(lanes >= rows + 8 * b, a[b] * scale, 0.0)
        inverse_rows.append(q[b] * scale)
    inverse = jnp.concatenate(inverse_rows, axis=0)
    matrix = mat_ref[...].reshape(-1, k)
    basis = lax.dot_general(
        matrix, inverse, (((1,), (1,)), ((), ())), precision=HIGHEST, preferred_element_type=jnp.float32
    )
    basis_out[...] = basis.reshape(basis_out.shape)


def body(positions, velocities, masses, tangents):
    n, k = positions.shape[1], tangents.shape[2]
    xs, zs = lax.axis_size("blk") // 4, lax.axis_size("lane") // 2
    planes = xs * Y
    total = float(n * planes * zs * 2)
    targets, sources = planes * n, 2 * zs * n
    f32, bf16 = jnp.float32, jnp.bfloat16
    vmem = pl.BlockSpec(memory_space=pltpu.VMEM)
    dma = pltpu.SemaphoreType.DMA
    part_rows = 64 // planes
    scratch = [
        pltpu.VMEM((3, n), f32),
        pltpu.VMEM((3, n), f32),
        pltpu.VMEM((1, n), f32),
        pltpu.VMEM((6, n, k), f32),
        dma((4,)),
        pltpu.VMEM((planes, 4, 128), f32),
        pltpu.VMEM((2, zs, 3 * n + 8, k), f32),
        pltpu.VMEM((4, sources), f32),
        pltpu.VMEM((3, targets, 128), f32),
        pltpu.VMEM((3 * targets, 3 * sources), bf16),
        pltpu.VMEM((3 * targets, 3 * sources), bf16),
        pltpu.VMEM((3 * sources, 2 * k), bf16),
        pltpu.VMEM((9, targets, 128), f32),
        pltpu.VMEM((planes, 8, 128), f32),
        pltpu.VMEM((planes - 1, 8, 128), f32),
        pltpu.VMEM((planes // 2, 3, 2, n, k), f32),
        pltpu.VMEM((planes - 1, 3, n, k), f32),
        pltpu.VMEM((2 * planes, part_rows, k), f32),
        pltpu.VMEM((2 * planes - 1, part_rows, k), f32),
        pltpu.VMEM((part_rows, k), f32),
        pltpu.VMEM((zs - 1, part_rows, k), f32),
        pltpu.VMEM((2 * planes, part_rows, k), f32),
        dma, dma,
        dma((zs,)), dma((zs,)),
        dma((zs,)), dma((zs,)),
        dma, dma, dma, dma, dma((3,)), dma((3,)),
    ]
    gram, matrix, npos, nvel = pl.pallas_call(
        functools.partial(step_kernel, xs, zs, n, total),
        out_shape=[
            jax.ShapeDtypeStruct((k, k), f32),
            jax.ShapeDtypeStruct((6, n, k), f32),
            jax.ShapeDtypeStruct((3, n), f32),
            jax.ShapeDtypeStruct((3, n), f32),
        ],
        in_specs=[pl.BlockSpec(memory_space=pltpu.HBM)] * 4,
        out_specs=[vmem] * 4,
        scratch_shapes=scratch,
        compiler_params=pltpu.CompilerParams(
            collective_id=0, has_side_effects=True, vmem_limit_bytes=40 * 1024 * 1024
        ),
    )(*[
        pltpu.with_memory_space_constraint(array, pltpu.HBM)
        for array in (positions, velocities, masses.reshape(1, n), tangents)
    ])
    npos, nvel, basis, growth = pl.pallas_call(
        factor_kernel,
        out_shape=[
            jax.ShapeDtypeStruct((3, n), f32),
            jax.ShapeDtypeStruct((3, n), f32),
            jax.ShapeDtypeStruct((6, n, k), f32),
            jax.ShapeDtypeStruct((k, k), f32),
        ],
        in_specs=[vmem] * 4,
        out_specs=[vmem] * 4,
        compiler_params=pltpu.CompilerParams(vmem_limit_bytes=40 * 1024 * 1024),
    )(gram, matrix, npos, nvel)
    return (npos, nvel, basis, growth)


def solution(mesh):
    return jax.shard_map(
        body,
        mesh=mesh,
        in_specs=(
            P(None, ("blk", "lane")),
            P(None, ("blk", "lane")),
            P(("blk", "lane")),
            P(None, ("blk", "lane"), None),
        ),
        out_specs=(
            P(None, ("blk", "lane")),
            P(None, ("blk", "lane")),
            P(None, ("blk", "lane"), None),
            P(),
        ),
        check_vma=False,
    )
```
